512 devices in a mesh: lat: 32 (over z, core), lev: 16 (over x, y).
Axes of the slice: x: 4, y: 4, z: 16, core: 2. Of those that a mesh axis runs over, the one named last changes fastest.
Arguments:
- zonal_velocity: float32 [128, 512, 576], P('lev', 'lat'), may hold values from -6 to 6
- poleward_velocity: float32 [128, 512, 576], P('lev', 'lat'), may hold values from -6 to 6
- thermal_anomaly: float32 [128, 512, 576], P('lev', 'lat'), may hold values from -6 to 6
- scaled_humidity: float32 [128, 512, 576], P('lev', 'lat'), may hold values from 0 to 1
- ground_potential_energy: float32 [512, 576], P('lat'), may hold values from -6 to 6
- layer_depth_factor: float32 [128], replicated, may hold values from 0.02 to 0.2
Outputs:
- carried_heat_anomaly: float32 [128, 512, 576], P('lev', 'lat')
- carried_humidity: float32 [128, 512, 576], P('lev', 'lat')
- revised_zonal_velocity: float32 [128, 512, 576], P('lev', 'lat')
- revised_poleward_velocity: float32 [128, 512, 576], P('lev', 'lat')
- potential_altitude: float32 [128, 512, 576], P('lev', 'lat')
The draws below stay inside these ranges and needn't reach their ends.
All inputs are finite; a program needn't handle non-finite values.
Results may differ from the reference program's by a relative error of at most 0.00007.
Values sent between devices are 32-bit elements; how exact they have to be, the bound alone decides.
A program may use at most 64 MiB of HBM per device.

```python
import math
import jax
import jax.numpy as jnp

MERIDIAN_NUMBER = 576
PARALLEL_CIRCLES = 512
SIGMA_LAYERS = 128


def block_scale(own_key, shape, shards, low, top_value):
    gain, own = 1.0, jax.random.fold_in(own_key, 6)
    for position, blocks in shards:
        steps = jnp.exp(jax.random.uniform(jax.random.fold_in(own, position), (blocks,), jnp.float32, low / len(shards), top_value / len(shards)))
        gain = gain * jnp.repeat(steps, shape[position] // blocks).reshape([-1 if axis == position else 1 for axis in range(len(shape))])
    return gain


def scatter_about(own_key, dims, width, most, cuts=(), kind=jnp.bfloat16):
    drawn = jax.random.normal(own_key, dims, jnp.float32) * width
    if len(cuts) > 0:
        drawn = block_scale(own_key, dims, cuts, -0.22, 0.18) * drawn
    return jnp.clip(drawn, min=-most, max=most).astype(kind)


def setup_inputs(seed: int = 0) -> dict:
    streams_of = jax.random.split(jax.random.key(seed), 7)
    zonal_velocity = scatter_about(streams_of[0], (SIGMA_LAYERS, PARALLEL_CIRCLES, MERIDIAN_NUMBER), 1.0, 6.0, ((0, 16), (1, 32)), jnp.float32)
    poleward_velocity = scatter_about(streams_of[1], (SIGMA_LAYERS, PARALLEL_CIRCLES, MERIDIAN_NUMBER), 1.0, 6.0, ((0, 16), (1, 32)), jnp.float32)
    thermal_anomaly = scatter_about(streams_of[2], (SIGMA_LAYERS, PARALLEL_CIRCLES, MERIDIAN_NUMBER), 1.0, 6.0, ((0, 16), (1, 32)), jnp.float32)
    scaled_humidity = jnp.clip(1.0 * jax.random.uniform(streams_of[3], (SIGMA_LAYERS, PARALLEL_CIRCLES, MERIDIAN_NUMBER), jnp.float32) ** block_scale(streams_of[3], (SIGMA_LAYERS, PARALLEL_CIRCLES, MERIDIAN_NUMBER), ((0, 16), (1, 32)), -0.2, 0.2), 0.0, 1.0)
    ground_potential_energy = scatter_about(streams_of[4], (PARALLEL_CIRCLES, MERIDIAN_NUMBER), 1.0, 6.0, ((0, 32),), jnp.float32)
    layer_depth_factor = jnp.clip(jnp.exp(jax.random.uniform(streams_of[5], (SIGMA_LAYERS,), jnp.float32, math.log(0.02), math.log(0.2))), 0.02, 0.2)
    return dict(zonal_velocity=zonal_velocity, poleward_velocity=poleward_velocity, thermal_anomaly=thermal_anomaly, scaled_humidity=scaled_humidity, ground_potential_energy=ground_potential_energy, layer_depth_factor=layer_depth_factor)


ZONAL_RATE = 0.1
MERID_RATE = 0.25
POLAR_CAP = 0.2
MOIST_CORRECTION = 0.6


def lat_weights(row_index, circle_sum):
    spacing = jnp.pi / circle_sum
    middle_boxes = jnp.cos(-jnp.pi / 2 + (row_index + 0.5) * spacing)
    upper_interface = jnp.where(row_index + 1.0 < circle_sum, jnp.cos(-jnp.pi / 2 + (row_index + 1.0) * spacing), 0.0)
    lower_interface = jnp.where(row_index > 0.5, jnp.cos(-jnp.pi / 2 + row_index * spacing), 0.0)
    return middle_boxes[:, None], upper_interface[:, None], lower_interface[:, None]


def transport_scalar(tracer, tracer_south, tracer_north, zonal, merid, poleward_velocity_lower, poleward_velocity_upper, middle_boxes, upper_interface, lower_interface):
    zonal_coef = ZONAL_RATE / jnp.maximum(middle_boxes, POLAR_CAP)
    east_flux = 0.25 * (zonal + jnp.roll(zonal, -1, 2)) * (tracer + jnp.roll(tracer, -1, 2))
    zonal_div = east_flux - jnp.roll(east_flux, 1, 2)
    north_flux = upper_interface * 0.25 * (merid + poleward_velocity_upper) * (tracer + tracer_north)
    south_flux = lower_interface * 0.25 * (merid + poleward_velocity_lower) * (tracer + tracer_south)
    return tracer - zonal_coef * zonal_div - MERID_RATE / middle_boxes * (north_flux - south_flux)


def update_winds(zonal, merid, potential_altitude, height_south, height_north, middle_boxes):
    zonal_coef = 0.5 * ZONAL_RATE / jnp.maximum(middle_boxes, POLAR_CAP)
    revised_zonal_velocity = zonal - zonal_coef * (jnp.roll(potential_altitude, -1, 2) - jnp.roll(potential_altitude, 1, 2))
    revised_poleward_velocity = merid - 0.5 * MERID_RATE * (height_north - height_south)
    return revised_zonal_velocity, revised_poleward_velocity


def neighbour_boxes(field):
    empty = jnp.zeros_like(field[:, :1])
    north = jnp.concatenate([field[:, 1:], empty], axis=1)
    south = jnp.concatenate([empty, field[:, :-1]], axis=1)
    return south, north


def reference(zonal_velocity, poleward_velocity, thermal_anomaly, scaled_humidity, ground_potential_energy, layer_depth_factor):
    circle_sum = thermal_anomaly.shape[1]
    row_index = jnp.arange(circle_sum).astype(jnp.float32)
    middle_boxes, upper_interface, lower_interface = lat_weights(row_index, circle_sum)
    poleward_velocity_lower, poleward_velocity_upper = neighbour_boxes(poleward_velocity)
    thermal_anomaly_equatorward, thermal_anomaly_poleward = neighbour_boxes(thermal_anomaly)
    moist_south, moist_north = neighbour_boxes(scaled_humidity)
    carried_heat_anomaly = transport_scalar(thermal_anomaly, thermal_anomaly_equatorward, thermal_anomaly_poleward, zonal_velocity, poleward_velocity, poleward_velocity_lower, poleward_velocity_upper, middle_boxes, upper_interface, lower_interface)
    carried_humidity = transport_scalar(scaled_humidity, moist_south, moist_north, zonal_velocity, poleward_velocity, poleward_velocity_lower, poleward_velocity_upper, middle_boxes, upper_interface, lower_interface)
    density_adjusted_heat = carried_heat_anomaly + MOIST_CORRECTION * carried_humidity
    weighted = layer_depth_factor[:, None, None] * density_adjusted_heat
    below = jnp.flip(jnp.cumsum(jnp.flip(weighted, 0), 0), 0)
    potential_altitude = ground_potential_energy[None] + below
    height_south, height_north = neighbour_boxes(potential_altitude)
    revised_zonal_velocity, revised_poleward_velocity = update_winds(zonal_velocity, poleward_velocity, potential_altitude, height_south, height_north, middle_boxes)
    return carried_heat_anomaly, carried_humidity, revised_zonal_velocity, revised_poleward_velocity, potential_altitude
```

```python
import functools
import jax
import jax.numpy as jnp
from jax import lax
from jax.experimental import pallas as pl
from jax.experimental.pallas import tpu as pltpu
from jax.sharding import PartitionSpec as P

ZONAL_RATE = 0.1
MERID_RATE = 0.25
POLAR_CAP = 0.2
MOIST_CORRECTION = 0.6
F32 = jnp.float32
MESH = pl.DeviceIdType.MESH


def lat_weights(row_index, circle_sum):
    spacing = jnp.pi / circle_sum
    middle_boxes = jnp.cos(-jnp.pi / 2 + (row_index + 0.5) * spacing)
    upper_interface = jnp.where(
        row_index + 1.0 < circle_sum, jnp.cos(-jnp.pi / 2 + (row_index + 1.0) * spacing), 0.0
    )
    lower_interface = jnp.where(row_index > 0.5, jnp.cos(-jnp.pi / 2 + row_index * spacing), 0.0)
    return middle_boxes, upper_interface, lower_interface


def widen(column, width):
    whole, rest = width // 128, width % 128
    parts = [column] * whole + ([column[:, :rest]] if rest else [])
    return jnp.concatenate(parts, axis=1)


def wrapped(value):
    width = value.shape[1]
    extra = -width % 128
    if extra == 0:
        return value
    return jnp.concatenate([value, value[:, :extra]], axis=1)


def east(full):
    return pltpu.roll(full, full.shape[1] - 1, 1)


def west(full, width):
    size = full.shape[1]
    rolled = pltpu.roll(full, 1, 1)
    if size == width:
        return rolled
    last = pltpu.roll(full[:, size - 128 :], 128 - (width - 1 - (size - 128)), 1)
    lane = lax.broadcasted_iota(jnp.int32, last.shape, 1)
    start = jnp.where(lane == 0, last, rolled[:, :128])
    return jnp.concatenate([start, rolled[:, 128:]], axis=1)


def advect_kernel(
    u_hbm, v_hbm, t_hbm, q_hbm, g_hbm, w_hbm,
    t_out, q_out, u_out, v_out, c_out, b_out,
    u_ref, v_ref, t_ref, q_ref, g_ref, w_ref,
    raw_send, raw_recv, part_send, part_recv,
    early_send, early_recv, late_send, late_recv, flux_ref, edge_ref,
    in_sem, raw_ssem, raw_rsem, part_ssem, part_rsem,
    early_ssem, early_rsem, late_ssem, late_rsem,
):
    lat, lev = lax.axis_index("lat"), lax.axis_index("lev")
    lats, levs = lax.axis_size("lat"), lax.axis_size("lev")
    levels, rows, width = t_ref.shape
    circle_sum = rows * lats
    full = width + (-width % 128)
    has_south, has_north = lat > 0, lat < lats - 1

    barrier = pltpu.get_barrier_semaphore()

    @pl.when(has_south)
    def _():
        pl.semaphore_signal(barrier, inc=1, device_id=(lat - 1, lev), device_id_type=MESH)

    @pl.when(has_north)
    def _():
        pl.semaphore_signal(barrier, inc=1, device_id=(lat + 1, lev), device_id_type=MESH)

    def greet(step, carry):
        pl.semaphore_signal(barrier, inc=1, device_id=(lat, lev + 1 + step), device_id_type=MESH)
        return carry

    lax.fori_loop(0, levs - 1 - lev, greet, 0)

    loads = [
        pltpu.make_async_copy(source, target, in_sem.at[n])
        for n, (source, target) in enumerate(
            [(t_hbm, t_ref), (q_hbm, q_ref), (v_hbm, v_ref), (u_hbm, u_ref), (g_hbm, g_ref), (w_hbm, w_ref)]
        )
    ]
    for load in loads:
        load.start()

    band = (lat * rows + lax.broadcasted_iota(jnp.int32, (rows, 128), 0)).astype(F32)
    centre, upper, lower = lat_weights(band, circle_sum)
    zonal = ZONAL_RATE / jnp.maximum(centre, POLAR_CAP)
    merid = MERID_RATE / centre
    beside = lat * rows - 1 + (rows + 1) * lax.broadcasted_iota(jnp.int32, (8, 128), 0)
    beside_centre, _, _ = lat_weights(beside.astype(F32), circle_sum)
    merid_beside = MERID_RATE / beside_centre
    south_interface, north_interface = lower[0:1], upper[rows - 1 :]
    merid_south, merid_north = merid_beside[0:1], merid_beside[1:2]
    row_of = lax.broadcasted_iota(jnp.int32, (rows, width), 0)
    upper_wide = widen(upper, width)
    zonal_wide, merid_wide = widen(zonal, width), widen(merid, width)

    def packed(ref, row):
        return ref[:, row, :]

    def spread(row):
        return widen(jnp.broadcast_to(row, (levels, 128)), width)

    if lats > 1:
        @pl.when(jnp.logical_not(has_north))
        def _():
            raw_recv[0] = jnp.zeros(raw_recv.shape[1:], F32)
            part_recv[0] = jnp.zeros(part_recv.shape[1:], F32)

        @pl.when(jnp.logical_not(has_south))
        def _():
            raw_recv[1] = jnp.zeros(raw_recv.shape[1:], F32)
            part_recv[1] = jnp.zeros(part_recv.shape[1:], F32)

    for load in loads[:3]:
        load.wait()

    for side, row in ((0, 0), (1, rows - 1)):
        raw_send[side, 0] = packed(v_ref, row)
        raw_send[side, 1] = packed(t_ref, row)
        raw_send[side, 2] = packed(q_ref, row)
    pl.semaphore_wait(
        barrier, lev + has_south.astype(jnp.int32) + has_north.astype(jnp.int32)
    )

    def halo(send, recv, ssem, rsem, side):
        return pltpu.make_async_remote_copy(
            src_ref=send.at[side],
            dst_ref=recv.at[side],
            send_sem=ssem.at[side],
            recv_sem=rsem.at[side],
            device_id=(lat - 1 if side == 0 else lat + 1, lev),
            device_id_type=MESH,
        )

    raw_copies = [halo(raw_send, raw_recv, raw_ssem, raw_rsem, side) for side in (0, 1)]
    part_copies = [halo(part_send, part_recv, part_ssem, part_rsem, side) for side in (0, 1)]
    pl.when(has_south)(raw_copies[0].start)
    pl.when(has_north)(raw_copies[1].start)

    for load in loads[3:]:
        load.wait()

    for side, row, inner, interface, sign in (
        (0, 0, 1, upper[0:1], -1.0),
        (1, rows - 1, rows - 2, lower[rows - 1 :], 1.0),
    ):
        tracer = raw_send[side, 1] + MOIST_CORRECTION * raw_send[side, 2]
        tracer_in = packed(t_ref, inner) + MOIST_CORRECTION * packed(q_ref, inner)
        wind_in = packed(v_ref, inner)
        flux_in = spread(interface * 0.25) * (raw_send[side, 0] + wind_in) * (tracer + tracer_in)
        wind = wrapped(packed(u_ref, row))
        around = wrapped(tracer)
        flux = 0.25 * (wind + east(wind)) * (around + east(around))
        change = (flux - west(flux, width))[:, :width]
        part_send[side, 0] = (
            tracer
            - spread(zonal[row : row + 1]) * change
            + sign * spread(merid[row : row + 1]) * flux_in
        )
        part_send[side, 1] = jnp.broadcast_to(g_ref[row : row + 1, :], (levels, width))
    pl.when(has_south)(part_copies[0].start)
    pl.when(has_north)(part_copies[1].start)

    def partial(k, carry):
        zonal_sum, merid_sum, own_sum = carry
        weight = w_ref[lev * levels + k]
        tracer = t_ref[k] + MOIST_CORRECTION * q_ref[k]
        around = wrapped(tracer)
        wind = wrapped(u_ref[k])
        zonal_sum += weight * ((wind + east(wind)) * (around + east(around)))
        cross = v_ref[k]
        merid_sum += weight * (
            (cross + pltpu.roll(cross, rows - 1, 0)) * (tracer + pltpu.roll(tracer, rows - 1, 0))
        )
        return zonal_sum, merid_sum, own_sum + weight * tracer

    zonal_sum, merid_sum, own_sum = lax.fori_loop(
        0,
        levels,
        partial,
        (jnp.zeros((rows, full), F32), jnp.zeros((rows, width), F32), jnp.zeros((rows, width), F32)),
    )
    north_sum = jnp.where(row_of < rows - 1, 0.25 * upper_wide * merid_sum, 0.0)
    early_send[...] = (
        own_sum
        - zonal_wide * (0.25 * (zonal_sum - west(zonal_sum, width)))[:, :width]
        - merid_wide * (north_sum - pltpu.roll(north_sum, 1, 0))
    )

    def exchange(send, recv, ssem, rsem, other):
        return pltpu.make_async_remote_copy(
            src_ref=send,
            dst_ref=recv.at[lev],
            send_sem=ssem.at[other],
            recv_sem=rsem.at[lev],
            device_id=(lat, other),
            device_id_type=MESH,
        )

    def send_early(other, carry):
        exchange(early_send, early_recv, early_ssem, early_rsem, other).start()
        return carry

    lax.fori_loop(0, lev, send_early, 0)

    pl.when(has_south)(raw_copies[1].wait_recv)
    pl.when(has_north)(raw_copies[0].wait_recv)
    for side, interface in ((0, north_interface), (1, south_interface)):
        mine = 1 - side
        wind = spread(interface * 0.25) * (raw_send[mine, 0] + raw_recv[side, 0])
        flux_ref[side, 0] = wind * (raw_send[mine, 1] + raw_recv[side, 1])
        flux_ref[side, 1] = wind * (raw_send[mine, 2] + raw_recv[side, 2])
    level_of = lax.broadcasted_iota(jnp.int32, (levels, 128), 0)
    weights = jnp.zeros((levels, 128), F32)
    for k in range(levels):
        weights = jnp.where(level_of == k, w_ref[lev * levels + k], weights)
    weights = widen(weights, width)
    pl.when(has_south)(part_copies[1].wait_recv)
    pl.when(has_north)(part_copies[0].wait_recv)
    for side, exists, merid_edge, sign in (
        (0, has_north, merid_north, 1.0),
        (1, has_south, merid_south, -1.0),
    ):
        flux = flux_ref[side, 0] + MOIST_CORRECTION * flux_ref[side, 1]
        part = part_recv[side, 0]
        late_send[side : side + 1] = jnp.sum(weights * flux, axis=0, keepdims=True)
        late_send[side + 2 : side + 3] = jnp.sum(weights * part, axis=0, keepdims=True)
        beyond = weights * (part + sign * spread(merid_edge) * flux)
        edge_ref[side] = jnp.where(exists, beyond, 0.0)

    def send_late(other, carry):
        exchange(late_send, late_recv, late_ssem, late_rsem, other).start()
        return carry

    lax.fori_loop(0, lev, send_late, 0)

    half_zonal = 0.5 * zonal_wide

    def local(step, carry):
        below, below_north, below_south = carry
        k = levels - 1 - step
        weight = w_ref[lev * levels + k]
        wind, cross = u_ref[k], v_ref[k]
        wind_full = wrapped(wind)
        wind_pair = 0.25 * (wind_full + east(wind_full))
        cross_pair = 0.25 * upper_wide * (cross + pltpu.roll(cross, rows - 1, 0))

        def moved(tracer, kind):
            around = wrapped(tracer)
            flux = wind_pair * (around + east(around))
            change = (flux - west(flux, width))[:, :width]
            inner = cross_pair * (tracer + pltpu.roll(tracer, rows - 1, 0))
            north = jnp.where(row_of == rows - 1, flux_ref[0, kind, pl.ds(k, 1), :], inner)
            south = jnp.where(row_of == 0, flux_ref[1, kind, pl.ds(k, 1), :], pltpu.roll(inner, 1, 0))
            return tracer - zonal_wide * change - merid_wide * (north - south)

        heat, humid = moved(t_ref[k], 0), moved(q_ref[k], 1)
        t_out[k] = heat
        q_out[k] = humid
        below = below + weight * (heat + MOIST_CORRECTION * humid)
        below_north = below_north + edge_ref[0, pl.ds(k, 1), :]
        below_south = below_south + edge_ref[1, pl.ds(k, 1), :]
        c_out[k] = below
        around = wrapped(below)
        u_out[k] = wind - half_zonal * (east(around) - west(around, width))[:, :width]
        north = jnp.where(row_of == rows - 1, below_north, pltpu.roll(below, rows - 1, 0))
        south = jnp.where(row_of == 0, below_south, pltpu.roll(below, 1, 0))
        v_out[k] = cross - 0.5 * MERID_RATE * (north - south)
        return below, below_north, below_south

    lax.fori_loop(
        0,
        levels,
        local,
        (jnp.zeros((rows, width), F32), jnp.zeros((1, width), F32), jnp.zeros((1, width), F32)),
    )

    def add_early(other, total):
        pltpu.make_async_copy(early_recv.at[other], early_recv.at[other], early_rsem.at[other]).wait()
        return total + early_recv[other]

    def add_late(other, total):
        pltpu.make_async_copy(late_recv.at[other], late_recv.at[other], late_rsem.at[other]).wait()
        return total + late_recv[other]

    total = lax.fori_loop(lev + 1, levs, add_early, g_ref[...])
    edges = lax.fori_loop(lev + 1, levs, add_late, jnp.zeros(late_send.shape, F32))
    north_flux, south_flux = edges[0:1], edges[1:2]
    total = total + merid_wide * (
        jnp.where(row_of == 0, south_flux, 0.0) - jnp.where(row_of == rows - 1, north_flux, 0.0)
    )
    beyond_north = part_recv[0, 1, 0:1] + edges[2:3] + widen(merid_north, width) * north_flux
    beyond_south = part_recv[1, 1, 0:1] + edges[3:4] - widen(merid_south, width) * south_flux
    beyond_north = jnp.where(has_north, beyond_north, 0.0)
    beyond_south = jnp.where(has_south, beyond_south, 0.0)
    around = wrapped(total)
    b_out[0] = total
    b_out[1] = half_zonal * (east(around) - west(around, width))[:, :width]
    north = jnp.where(row_of == rows - 1, beyond_north, pltpu.roll(total, rows - 1, 0))
    south = jnp.where(row_of == 0, beyond_south, pltpu.roll(total, 1, 0))
    b_out[2] = 0.5 * MERID_RATE * (north - south)

    for side, exists in ((0, has_south), (1, has_north)):
        pl.when(exists)(raw_copies[side].wait_send)
        pl.when(exists)(part_copies[side].wait_send)

    def sent(other, carry):
        exchange(early_send, early_recv, early_ssem, early_rsem, other).wait_send()
        exchange(late_send, late_recv, late_ssem, late_rsem, other).wait_send()
        return carry

    lax.fori_loop(0, lev, sent, 0)


def finish_kernel(t_in, q_in, u_in, v_in, c_in, b_in, t, q, u, v, h, u_new, v_new, h_new, sems):
    copies = [
        pltpu.make_async_copy(source, target, sems.at[n])
        for n, (source, target) in enumerate([(t_in, t), (q_in, q), (h_new, h), (u_new, u), (v_new, v)])
    ]
    copies[0].start()
    copies[1].start()
    for k in range(t_in.shape[0]):
        h_new[k] = c_in[k] + b_in[0]
    copies[2].start()
    for k in range(t_in.shape[0]):
        u_new[k] = u_in[k] - b_in[1]
    copies[3].start()
    for k in range(t_in.shape[0]):
        v_new[k] = v_in[k] - b_in[2]
    copies[4].start()
    for copy in copies:
        copy.wait()


def body(zonal, poleward, heat, humidity, ground, weights):
    levels, rows, width = heat.shape
    levs = lax.axis_size("lev")
    slab = (levels, rows, width)
    anywhere = pl.BlockSpec(memory_space=pl.ANY)
    vmem = pl.BlockSpec(memory_space=pltpu.VMEM)
    dma = pltpu.SemaphoreType.DMA
    args = [pltpu.with_memory_space_constraint(x, pltpu.HBM) for x in (zonal, poleward, heat, humidity, ground, weights)]
    parts = pl.pallas_call(
        advect_kernel,
        name="advect",
        out_shape=[pltpu.VMEM(slab, F32)] * 5 + [pltpu.VMEM((3, rows, width), F32)],
        in_specs=[anywhere] * 6,
        out_specs=[vmem] * 6,
        scratch_shapes=[pltpu.VMEM(slab, F32)] * 4
        + [
            pltpu.VMEM((rows, width), F32),
            pltpu.SMEM(weights.shape, F32),
            pltpu.VMEM((2, 3, levels, width), F32),
            pltpu.VMEM((2, 3, levels, width), F32),
            pltpu.VMEM((2, 2, levels, width), F32),
            pltpu.VMEM((2, 2, levels, width), F32),
            pltpu.VMEM((rows, width), F32),
            pltpu.VMEM((levs, rows, width), F32),
            pltpu.VMEM((4, width), F32),
            pltpu.VMEM((levs, 4, width), F32),
            pltpu.VMEM((2, 2, levels, width), F32),
            pltpu.VMEM((2, levels, width), F32),
            dma((6,)),
            dma((2,)),
            dma((2,)),
            dma((2,)),
            dma((2,)),
            dma((levs,)),
            dma((levs,)),
            dma((levs,)),
            dma((levs,)),
        ],
        compiler_params=pltpu.CompilerParams(
            collective_id=0, has_side_effects=True, vmem_limit_bytes=32 * 2**20
        ),
    )(*args)
    return pl.pallas_call(
        finish_kernel,
        name="finish",
        out_shape=[jax.ShapeDtypeStruct(slab, F32)] * 5,
        in_specs=[vmem] * 6,
        out_specs=[anywhere] * 5,
        scratch_shapes=[pltpu.VMEM(slab, F32)] * 3 + [dma((5,))],
        compiler_params=pltpu.CompilerParams(vmem_limit_bytes=16 * 2**20),
    )(*parts)


def solution(mesh):
    slab = P("lev", "lat", None)
    return jax.shard_map(
        body,
        mesh=mesh,
        in_specs=(slab,) * 4 + (P("lat", None), P()),
        out_specs=(slab,) * 5,
        check_vma=False,
    )
```

```python
import functools
import jax
import jax.numpy as jnp
from jax import lax
from jax.experimental import pallas as pl
from jax.experimental.pallas import tpu as pltpu
from jax.sharding import PartitionSpec as P

ZONAL_RATE = 0.1
MERID_RATE = 0.25
POLAR_CAP = 0.2
MOIST_CORRECTION = 0.6
F32 = jnp.float32
MESH = pl.DeviceIdType.MESH


def lat_weights(row_index, circle_sum):
    spacing = jnp.pi / circle_sum
    middle_boxes = jnp.cos(-jnp.pi / 2 + (row_index + 0.5) * spacing)
    upper_interface = jnp.where(
        row_index + 1.0 < circle_sum, jnp.cos(-jnp.pi / 2 + (row_index + 1.0) * spacing), 0.0
    )
    lower_interface = jnp.where(row_index > 0.5, jnp.cos(-jnp.pi / 2 + row_index * spacing), 0.0)
    return middle_boxes, upper_interface, lower_interface


def widen(column, width):
    whole, rest = width // 128, width % 128
    parts = [column] * whole + ([column[:, :rest]] if rest else [])
    return jnp.concatenate(parts, axis=1)


def wrapped(value):
    width = value.shape[1]
    extra = -width % 128
    if extra == 0:
        return value
    return jnp.concatenate([value, value[:, :extra]], axis=1)


def east(full):
    return pltpu.roll(full, full.shape[1] - 1, 1)


def west(full, width):
    size = full.shape[1]
    rolled = pltpu.roll(full, 1, 1)
    if size == width:
        return rolled
    last = pltpu.roll(full[:, size - 128 :], 128 - (width - 1 - (size - 128)), 1)
    lane = lax.broadcasted_iota(jnp.int32, last.shape, 1)
    start = jnp.where(lane == 0, last, rolled[:, :128])
    return jnp.concatenate([start, rolled[:, 128:]], axis=1)


def advect_kernel(
    u_hbm, v_hbm, t_hbm, q_hbm, g_hbm, w_hbm,
    t_out, q_out, u_out, v_out, c_out, b_out,
    u_ref, v_ref, t_ref, q_ref, g_ref, w_ref,
    first_send, first_recv, rows_send, rows_recv, rest_send, rest_recv,
    sum_send, meet_y, meet_x, total_send, pair_send, far_x, far_y,
    late_send, late_recv, flux_ref, edge_ref,
    in_sem, halo_ssem, halo_rsem, y_ssem, y_rsem, x_ssem, x_rsem, late_ssem, late_rsem,
):
    lat, lev = lax.axis_index("lat"), lax.axis_index("lev")
    lats, levs = lax.axis_size("lat"), lax.axis_size("lev")
    along_y = meet_y.shape[0]
    x, y = lev // along_y, lev % along_y
    levels, rows, width = t_ref.shape
    half = rows // 2
    circle_sum = rows * lats
    full = width + (-width % 128)
    has_south, has_north = lat > 0, lat < lats - 1

    barrier = pltpu.get_barrier_semaphore()

    def greet(band, slab):
        pl.semaphore_signal(barrier, inc=1, device_id=(band, slab), device_id_type=MESH)

    @pl.when(has_south)
    def _():
        greet(lat - 1, lev)

    @pl.when(has_north)
    def _():
        greet(lat + 1, lev)

    lax.fori_loop(0, levs - 1 - lev, lambda step, c: (greet(lat, lev + 1 + step), c)[1], 0)
    lax.fori_loop(0, y, lambda step, c: (greet(lat, x * along_y + step), c)[1], 0)

    loads = [
        pltpu.make_async_copy(source, target, in_sem.at[n])
        for n, (source, target) in enumerate(
            [(v_hbm, v_ref), (t_hbm, t_ref), (q_hbm, q_ref), (u_hbm, u_ref), (g_hbm, g_ref), (w_hbm, w_ref)]
        )
    ]
    for load in loads:
        load.start()

    band = (lat * rows + lax.broadcasted_iota(jnp.int32, (rows, 128), 0)).astype(F32)
    centre, upper, lower = lat_weights(band, circle_sum)
    zonal = ZONAL_RATE / jnp.maximum(centre, POLAR_CAP)
    merid = MERID_RATE / centre
    beside = lat * rows - 1 + (rows + 1) * lax.broadcasted_iota(jnp.int32, (8, 128), 0)
    beside_centre, _, _ = lat_weights(beside.astype(F32), circle_sum)
    merid_beside = MERID_RATE / beside_centre
    south_interface, north_interface = lower[0:1], upper[rows - 1 :]
    merid_south, merid_north = merid_beside[0:1], merid_beside[1:2]
    row_of = lax.broadcasted_iota(jnp.int32, (rows, width), 0)
    upper_wide = widen(upper, width)
    zonal_wide, merid_wide = widen(zonal, width), widen(merid, width)

    def spread(row):
        return widen(jnp.broadcast_to(row, (levels, 128)), width)

    for side, exists in ((0, has_north), (1, has_south)):

        @pl.when(jnp.logical_not(exists))
        def _(side=side):
            first_recv[side] = jnp.zeros(first_recv.shape[1:], F32)
            rows_recv[side] = jnp.zeros(rows_recv.shape[1:], F32)
            rest_recv[side] = jnp.zeros(rest_recv.shape[1:], F32)

    def halo(kind, send, recv, side):
        return pltpu.make_async_remote_copy(
            src_ref=send.at[side],
            dst_ref=recv.at[side],
            send_sem=halo_ssem.at[kind, side],
            recv_sem=halo_rsem.at[kind, side],
            device_id=(lat - 1 if side == 0 else lat + 1, lev),
            device_id_type=MESH,
        )

    halos = [
        [halo(kind, send, recv, side) for side in (0, 1)]
        for kind, (send, recv) in enumerate(
            [(first_send, first_recv), (rows_send, rows_recv), (rest_send, rest_recv)]
        )
    ]

    def start_halos(kind):
        pl.when(has_south)(halos[kind][0].start)
        pl.when(has_north)(halos[kind][1].start)

    def wait_halos(kind):
        pl.when(has_south)(halos[kind][1].wait_recv)
        pl.when(has_north)(halos[kind][0].wait_recv)

    for load in loads[:3]:
        load.wait()

    for side, row in ((0, 0), (1, rows - 1)):
        first_send[side, 0] = v_ref[:, row, :]
        first_send[side, 1] = t_ref[:, row, :] + MOIST_CORRECTION * q_ref[:, row, :]
    pl.semaphore_wait(
        barrier,
        lev + along_y - 1 - y + has_south.astype(jnp.int32) + has_north.astype(jnp.int32),
    )
    start_halos(0)

    for load in loads[3:]:
        load.wait()
    level_of = lax.broadcasted_iota(jnp.int32, (levels, 128), 0)
    weights = jnp.zeros((levels, 128), F32)
    for k in range(levels):
        weights = jnp.where(level_of == k, w_ref[lev * levels + k], weights)
    weights = widen(weights, width)

    for side, row, inner, interface, sign in (
        (0, 0, 1, upper[0:1], -1.0),
        (1, rows - 1, rows - 2, lower[rows - 1 :], 1.0),
    ):
        tracer = first_send[side, 1]
        tracer_in = t_ref[:, inner, :] + MOIST_CORRECTION * q_ref[:, inner, :]
        flux_in = (
            spread(interface * 0.25) * (first_send[side, 0] + v_ref[:, inner, :]) * (tracer + tracer_in)
        )
        wind = wrapped(u_ref[:, row, :])
        around = wrapped(tracer)
        flux = 0.25 * (wind + east(wind)) * (around + east(around))
        change = (flux - west(flux, width))[:, :width]
        part = (
            tracer
            - spread(zonal[row : row + 1]) * change
            + sign * spread(merid[row : row + 1]) * flux_in
        )
        rest_send[side, 2] = part
        rows_send[side, 0:1] = jnp.sum(weights * part, axis=0, keepdims=True)
        rows_send[side, 1:2] = g_ref[row : row + 1, :]
    start_halos(1)

    def partial(k, carry):
        zonal_sum, merid_sum, own_sum = carry
        weight = w_ref[lev * levels + k]
        tracer = t_ref[k] + MOIST_CORRECTION * q_ref[k]
        around = wrapped(tracer)
        wind = wrapped(u_ref[k])
        zonal_sum += weight * ((wind + east(wind)) * (around + east(around)))
        cross = v_ref[k]
        merid_sum += weight * (
            (cross + pltpu.roll(cross, rows - 1, 0)) * (tracer + pltpu.roll(tracer, rows - 1, 0))
        )
        return zonal_sum, merid_sum, own_sum + weight * tracer

    zonal_sum, merid_sum, own_sum = lax.fori_loop(
        0,
        levels,
        partial,
        (jnp.zeros((rows, full), F32), jnp.zeros((rows, width), F32), jnp.zeros((rows, width), F32)),
        unroll=True,
    )
    north_sum = jnp.where(row_of < rows - 1, 0.25 * upper_wide * merid_sum, 0.0)
    slab_sum = (
        own_sum
        - zonal_wide * (0.25 * (zonal_sum - west(zonal_sum, width)))[:, :width]
        - merid_wide * (north_sum - pltpu.roll(north_sum, 1, 0))
    )
    sum_send[0] = slab_sum[:half]
    sum_send[1] = slab_sum[half:]

    def to_y(turn, step, source, target):
        other = (y + step) % along_y
        return pltpu.make_async_remote_copy(
            src_ref=source,
            dst_ref=target.at[y],
            send_sem=y_ssem.at[turn, other],
            recv_sem=y_rsem.at[turn, y],
            device_id=(lat, x * along_y + other),
            device_id_type=MESH,
        )

    def to_x(turn, other, source, target):
        return pltpu.make_async_remote_copy(
            src_ref=source,
            dst_ref=target.at[x],
            send_sem=x_ssem.at[turn, other],
            recv_sem=x_rsem.at[turn, x],
            device_id=(lat, other * along_y + y),
            device_id_type=MESH,
        )

    def wait_slot(target, slot, sem):
        pltpu.make_async_copy(target.at[slot], target.at[slot], sem).wait()

    steps = sorted(range(1, along_y), key=lambda step: -min(step, along_y - step))
    meets_y = [to_y(0, step, sum_send.at[0], meet_y) for step in steps]
    for copy in meets_y:
        copy.start()
    lax.fori_loop(0, x, lambda other, c: (to_x(0, other, sum_send.at[1], meet_x).start(), c)[1], 0)

    for side, row in ((0, 0), (1, rows - 1)):
        rest_send[side, 0] = t_ref[:, row, :]
        rest_send[side, 1] = q_ref[:, row, :]
    start_halos(2)

    wait_halos(0)
    wait_halos(1)
    for side, interface in ((0, north_interface), (1, south_interface)):
        mine = 1 - side
        wind = spread(interface * 0.25) * (first_send[mine, 0] + first_recv[side, 0])
        flux = wind * (first_send[mine, 1] + first_recv[side, 1])
        late_send[side : side + 1] = jnp.sum(weights * flux, axis=0, keepdims=True)
        late_send[side + 2 : side + 3] = rows_recv[side, 0:1]

    def to_lower(other):
        return pltpu.make_async_remote_copy(
            src_ref=late_send,
            dst_ref=late_recv.at[lev],
            send_sem=late_ssem.at[other],
            recv_sem=late_rsem.at[lev],
            device_id=(lat, other),
            device_id_type=MESH,
        )

    lax.fori_loop(0, lev, lambda other, c: (to_lower(other).start(), c)[1], 0)

    below_y = jnp.zeros((half, width), F32)
    total_y = sum_send[0]
    for step in range(1, along_y):
        other = (y + step) % along_y
        wait_slot(meet_y, other, y_rsem.at[0, other])
        came = meet_y[other]
        total_y += came
        below_y += jnp.where(y + step < along_y, came, 0.0)
    total_send[...] = total_y
    lax.fori_loop(0, x, lambda other, c: (to_x(1, other, total_send, far_x).start(), c)[1], 0)

    def add_x(turn, target):
        def add(other, total):
            wait_slot(target, other, x_rsem.at[turn, other])
            return total + target[other]

        return add

    below_x = lax.fori_loop(x + 1, levs // along_y, add_x(0, meet_x), jnp.zeros((half, width), F32))
    pair_send[0] = below_x
    pair_send[1] = below_x + sum_send[1]
    fars_y = [to_y(1, step, pair_send.at[(y + step) // along_y], far_y) for step in steps]
    for copy in fars_y:
        copy.start()

    wait_halos(2)
    for side, exists, interface, merid_edge, sign in (
        (0, has_north, north_interface, merid_north, 1.0),
        (1, has_south, south_interface, merid_south, -1.0),
    ):
        mine = 1 - side
        wind = spread(interface * 0.25) * (first_send[mine, 0] + first_recv[side, 0])
        flux_ref[side, 0] = wind * (rest_send[mine, 0] + rest_recv[side, 0])
        flux_ref[side, 1] = wind * (rest_send[mine, 1] + rest_recv[side, 1])
        flux = flux_ref[side, 0] + MOIST_CORRECTION * flux_ref[side, 1]
        beyond = weights * (rest_recv[side, 2] + sign * spread(merid_edge) * flux)
        edge_ref[side] = jnp.where(exists, beyond, 0.0)
    half_zonal = 0.5 * zonal_wide

    def local(step, carry):
        below, below_north, below_south = carry
        k = levels - 1 - step
        weight = w_ref[lev * levels + k]
        wind, cross = u_ref[k], v_ref[k]
        wind_full = wrapped(wind)
        wind_pair = 0.25 * (wind_full + east(wind_full))
        cross_pair = 0.25 * upper_wide * (cross + pltpu.roll(cross, rows - 1, 0))

        def moved(tracer, kind):
            around = wrapped(tracer)
            flux = wind_pair * (around + east(around))
            change = (flux - west(flux, width))[:, :width]
            inner = cross_pair * (tracer + pltpu.roll(tracer, rows - 1, 0))
            north = jnp.where(row_of == rows - 1, flux_ref[0, kind, pl.ds(k, 1), :], inner)
            south = jnp.where(row_of == 0, flux_ref[1, kind, pl.ds(k, 1), :], pltpu.roll(inner, 1, 0))
            return tracer - zonal_wide * change - merid_wide * (north - south)

        heat, humid = moved(t_ref[k], 0), moved(q_ref[k], 1)
        t_out[k] = heat
        q_out[k] = humid
        below = below + weight * (heat + MOIST_CORRECTION * humid)
        below_north = below_north + edge_ref[0, pl.ds(k, 1), :]
        below_south = below_south + edge_ref[1, pl.ds(k, 1), :]
        c_out[k] = below
        around = wrapped(below)
        u_out[k] = wind - half_zonal * (east(around) - west(around, width))[:, :width]
        north = jnp.where(row_of == rows - 1, below_north, pltpu.roll(below, rows - 1, 0))
        south = jnp.where(row_of == 0, below_south, pltpu.roll(below, 1, 0))
        v_out[k] = cross - 0.5 * MERID_RATE * (north - south)
        return below, below_north, below_south

    lax.fori_loop(
        0,
        levels,
        local,
        (jnp.zeros((rows, width), F32), jnp.zeros((1, width), F32), jnp.zeros((1, width), F32)),
        unroll=2,
    )

    south_half = lax.fori_loop(x + 1, levs // along_y, add_x(1, far_x), below_y)
    north_half = below_x
    for step in range(1, along_y):
        other = (y + step) % along_y
        wait_slot(far_y, other, y_rsem.at[1, other])
        north_half += far_y[other]
    total = g_ref[...] + jnp.concatenate([south_half, north_half], axis=0)

    def add_late(other, total):
        wait_slot(late_recv, other, late_rsem.at[other])
        return total + late_recv[other]

    edges = lax.fori_loop(lev + 1, levs, add_late, jnp.zeros(late_send.shape, F32))
    north_flux, south_flux = edges[0:1], edges[1:2]
    total = total + merid_wide * (
        jnp.where(row_of == 0, south_flux, 0.0) - jnp.where(row_of == rows - 1, north_flux, 0.0)
    )
    beyond_north = rows_recv[0, 1:2] + edges[2:3] + widen(merid_north, width) * north_flux
    beyond_south = rows_recv[1, 1:2] + edges[3:4] - widen(merid_south, width) * south_flux
    beyond_north = jnp.where(has_north, beyond_north, 0.0)
    beyond_south = jnp.where(has_south, beyond_south, 0.0)
    around = wrapped(total)
    b_out[0] = total
    b_out[1] = half_zonal * (east(around) - west(around, width))[:, :width]
    north = jnp.where(row_of == rows - 1, beyond_north, pltpu.roll(total, rows - 1, 0))
    south = jnp.where(row_of == 0, beyond_south, pltpu.roll(total, 1, 0))
    b_out[2] = 0.5 * MERID_RATE * (north - south)

    for kind in range(3):
        pl.when(has_south)(halos[kind][0].wait_send)
        pl.when(has_north)(halos[kind][1].wait_send)
    for copy in meets_y + fars_y:
        copy.wait_send()
    lax.fori_loop(0, x, lambda other, c: (to_x(0, other, sum_send.at[1], meet_x).wait_send(), c)[1], 0)
    lax.fori_loop(0, x, lambda other, c: (to_x(1, other, total_send, far_x).wait_send(), c)[1], 0)
    lax.fori_loop(0, lev, lambda other, c: (to_lower(other).wait_send(), c)[1], 0)


def finish_kernel(t_in, q_in, u_in, v_in, c_in, b_in, t, q, u, v, h, u_new, v_new, h_new, sems):
    copies = [
        pltpu.make_async_copy(source, target, sems.at[n])
        for n, (source, target) in enumerate([(t_in, t), (q_in, q), (h_new, h), (u_new, u), (v_new, v)])
    ]
    copies[0].start()
    copies[1].start()
    for k in range(t_in.shape[0]):
        h_new[k] = c_in[k] + b_in[0]
    copies[2].start()
    for k in range(t_in.shape[0]):
        u_new[k] = u_in[k] - b_in[1]
    copies[3].start()
    for k in range(t_in.shape[0]):
        v_new[k] = v_in[k] - b_in[2]
    copies[4].start()
    for copy in copies:
        copy.wait()


def body(zonal, poleward, heat, humidity, ground, weights):
    levels, rows, width = heat.shape
    levs = lax.axis_size("lev")
    along_y = 4 if levs % 4 == 0 else levs
    along_x, half = levs // along_y, rows // 2
    slab = (levels, rows, width)
    anywhere = pl.BlockSpec(memory_space=pl.ANY)
    vmem = pl.BlockSpec(memory_space=pltpu.VMEM)
    dma = pltpu.SemaphoreType.DMA
    args = [pltpu.with_memory_space_constraint(x, pltpu.HBM) for x in (zonal, poleward, heat, humidity, ground, weights)]
    parts = pl.pallas_call(
        advect_kernel,
        name="advect",
        out_shape=[pltpu.VMEM(slab, F32)] * 5 + [pltpu.VMEM((3, rows, width), F32)],
        in_specs=[anywhere] * 6,
        out_specs=[vmem] * 6,
        scratch_shapes=[pltpu.VMEM(slab, F32)] * 4
        + [
            pltpu.VMEM((rows, width), F32),
            pltpu.SMEM(weights.shape, F32),
            pltpu.VMEM((2, 2, levels, width), F32),
            pltpu.VMEM((2, 2, levels, width), F32),
            pltpu.VMEM((2, 2, width), F32),
            pltpu.VMEM((2, 2, width), F32),
            pltpu.VMEM((2, 3, levels, width), F32),
            pltpu.VMEM((2, 3, levels, width), F32),
            pltpu.VMEM((2, half, width), F32),
            pltpu.VMEM((along_y, half, width), F32),
            pltpu.VMEM((along_x, half, width), F32),
            pltpu.VMEM((half, width), F32),
            pltpu.VMEM((2, half, width), F32),
            pltpu.VMEM((along_x, half, width), F32),
            pltpu.VMEM((along_y, half, width), F32),
            pltpu.VMEM((4, width), F32),
            pltpu.VMEM((levs, 4, width), F32),
            pltpu.VMEM((2, 2, levels, width), F32),
            pltpu.VMEM((2, levels, width), F32),
            dma((6,)),
            dma((3, 2)),
            dma((3, 2)),
            dma((2, along_y)),
            dma((2, along_y)),
            dma((2, along_x)),
            dma((2, along_x)),
            dma((levs,)),
            dma((levs,)),
        ],
        compiler_params=pltpu.CompilerParams(
            collective_id=0, has_side_effects=True, vmem_limit_bytes=32 * 2**20
        ),
    )(*args)
    return pl.pallas_call(
        finish_kernel,
        name="finish",
        out_shape=[jax.ShapeDtypeStruct(slab, F32)] * 5,
        in_specs=[vmem] * 6,
        out_specs=[anywhere] * 5,
        scratch_shapes=[pltpu.VMEM(slab, F32)] * 3 + [dma((5,))],
        compiler_params=pltpu.CompilerParams(vmem_limit_bytes=16 * 2**20),
    )(*parts)


def solution(mesh):
    slab = P("lev", "lat", None)
    return jax.shard_map(
        body,
        mesh=mesh,
        in_specs=(slab,) * 4 + (P("lat", None), P()),
        out_specs=(slab,) * 5,
        check_vma=False,
    )
```

```python
import functools
import jax
import jax.numpy as jnp
from jax import lax
from jax.experimental import pallas as pl
from jax.experimental.pallas import tpu as pltpu
from jax.sharding import PartitionSpec as P

ZONAL_RATE = 0.1
MERID_RATE = 0.25
POLAR_CAP = 0.2
MOIST_CORRECTION = 0.6
F32 = jnp.float32
MESH = pl.DeviceIdType.MESH


def lat_weights(row_index, circle_sum):
    spacing = jnp.pi / circle_sum
    middle_boxes = jnp.cos(-jnp.pi / 2 + (row_index + 0.5) * spacing)
    upper_interface = jnp.where(
        row_index + 1.0 < circle_sum, jnp.cos(-jnp.pi / 2 + (row_index + 1.0) * spacing), 0.0
    )
    lower_interface = jnp.where(row_index > 0.5, jnp.cos(-jnp.pi / 2 + row_index * spacing), 0.0)
    return middle_boxes, upper_interface, lower_interface


def widen(column, width):
    whole, rest = width // 128, width % 128
    parts = [column] * whole + ([column[:, :rest]] if rest else [])
    return jnp.concatenate(parts, axis=1)


def wrapped(value):
    width = value.shape[1]
    extra = -width % 128
    if extra == 0:
        return value
    return jnp.concatenate([value, value[:, :extra]], axis=1)


def east(full):
    return pltpu.roll(full, full.shape[1] - 1, 1)


def west(full, width):
    size = full.shape[1]
    rolled = pltpu.roll(full, 1, 1)
    if size == width:
        return rolled
    last = pltpu.roll(full[:, size - 128 :], 128 - (width - 1 - (size - 128)), 1)
    lane = lax.broadcasted_iota(jnp.int32, last.shape, 1)
    start = jnp.where(lane == 0, last, rolled[:, :128])
    return jnp.concatenate([start, rolled[:, 128:]], axis=1)


def advect_kernel(
    u_hbm, v_hbm, t_hbm, q_hbm, g_hbm, w_hbm,
    t_out, q_out, u_out, v_out, c_out, b_out,
    u_ref, v_ref, t_ref, q_ref, g_ref, w_ref, edge_rows,
    first_send, first_recv, rows_send, rows_recv, rest_send, rest_recv,
    sum_send, meet_y, total_send, far_x, meet_x, pair_send, far_y, hold_ref,
    late_send, late_recv,
    in_sem, edge_sem, halo_ssem, halo_rsem, y_ssem, y_rsem, x_ssem, x_rsem, late_ssem, late_rsem, ready,
):
    lat, lev = lax.axis_index("lat"), lax.axis_index("lev")
    lats, levs = lax.axis_size("lat"), lax.axis_size("lev")
    along_y = meet_y.shape[1]
    x, y = lev // along_y, lev % along_y
    levels, rows, width = t_ref.shape
    half = rows // 2
    circle_sum = rows * lats
    full = width + (-width % 128)
    has_south, has_north = lat > 0, lat < lats - 1

    barrier = pltpu.get_barrier_semaphore()
    first_band = lat == 0
    first = first_band & (lev == 0)

    def greet(band, slab):
        pl.semaphore_signal(barrier, inc=1, device_id=(band, slab), device_id_type=MESH)

    @pl.when(has_south)
    def _():
        greet(lat - 1, lev)

    @pl.when(has_north)
    def _():
        greet(lat + 1, lev)

    pl.when(first_band & (lev > 0))(lambda: greet(lat, 0))

    @pl.when(jnp.logical_not(first))
    def _():
        lax.fori_loop(lev + 1, levs, lambda slab, c: (greet(lat, slab), c)[1], 0)
        known = jnp.maximum(x * along_y, first_band.astype(jnp.int32))
        lax.fori_loop(known, lev, lambda slab, c: (greet(lat, slab), c)[1], 0)

    edge_loads = [
        pltpu.make_async_copy(
            source.at[:, pl.ds(side * (rows - 2), 2), :], edge_rows.at[kind, side], edge_sem.at[kind, side]
        )
        for kind, source in enumerate([v_hbm, t_hbm, q_hbm, u_hbm])
        for side in (0, 1)
    ]
    loads = [
        pltpu.make_async_copy(source, target, in_sem.at[n])
        for n, (source, target) in enumerate(
            [(w_hbm, w_ref), (g_hbm, g_ref), (t_hbm, t_ref), (q_hbm, q_ref), (u_hbm, u_ref), (v_hbm, v_ref)]
        )
    ]
    for load in edge_loads + loads[:2]:
        load.start()

    band = (lat * rows + lax.broadcasted_iota(jnp.int32, (rows, 128), 0)).astype(F32)
    centre, upper, lower = lat_weights(band, circle_sum)
    zonal = ZONAL_RATE / jnp.maximum(centre, POLAR_CAP)
    merid = MERID_RATE / centre
    beside = lat * rows - 1 + (rows + 1) * lax.broadcasted_iota(jnp.int32, (8, 128), 0)
    beside_centre, _, _ = lat_weights(beside.astype(F32), circle_sum)
    merid_beside = MERID_RATE / beside_centre
    south_interface, north_interface = lower[0:1], upper[rows - 1 :]
    merid_south, merid_north = merid_beside[0:1], merid_beside[1:2]
    row_of = lax.broadcasted_iota(jnp.int32, (rows, width), 0)
    upper_wide = widen(upper, width)
    zonal_wide, merid_wide = widen(zonal, width), widen(merid, width)

    def spread(row):
        return widen(jnp.broadcast_to(row, (levels, 128)), width)

    for side, exists in ((0, has_north), (1, has_south)):

        @pl.when(jnp.logical_not(exists))
        def _(side=side):
            first_recv[side] = jnp.zeros(first_recv.shape[1:], F32)
            rows_recv[side] = jnp.zeros(rows_recv.shape[1:], F32)
            rest_recv[side] = jnp.zeros(rest_recv.shape[1:], F32)

    def halo(kind, send, recv, side):
        return pltpu.make_async_remote_copy(
            src_ref=send.at[side],
            dst_ref=recv.at[side],
            send_sem=halo_ssem.at[kind, side],
            recv_sem=halo_rsem.at[kind, side],
            device_id=(lat - 1 if side == 0 else lat + 1, lev),
            device_id_type=MESH,
        )

    halos = [
        [halo(kind, send, recv, side) for side in (0, 1)]
        for kind, (send, recv) in enumerate(
            [(first_send, first_recv), (rows_send, rows_recv), (rest_send, rest_recv)]
        )
    ]

    def start_halos(kind):
        pl.when(has_south)(halos[kind][0].start)
        pl.when(has_north)(halos[kind][1].start)

    def wait_halos(kind):
        pl.when(has_south)(halos[kind][1].wait_recv)
        pl.when(has_north)(halos[kind][0].wait_recv)

    for load in edge_loads:
        load.wait()
    for load in loads[2:]:
        load.start()

    def edge_row(kind, side, inner=False):
        return edge_rows[kind, side, :, side if not inner else 1 - side, :]

    for side in (0, 1):
        first_send[side, 0] = edge_row(0, side)
        first_send[side, 1] = edge_row(1, side) + MOIST_CORRECTION * edge_row(2, side)
    pl.semaphore_wait(
        barrier,
        jnp.where(first, levs - 1, lev - first_band.astype(jnp.int32) + along_y - 1 - y)
        + has_south.astype(jnp.int32)
        + has_north.astype(jnp.int32),
    )
    start_halos(0)

    @pl.when(first)
    def _():
        def answer(slab, carry):
            pl.semaphore_signal(ready, inc=1, device_id=(lat, slab), device_id_type=MESH)
            return carry

        lax.fori_loop(1, levs, answer, 0)

    for load in loads[:2]:
        load.wait()
    level_of = lax.broadcasted_iota(jnp.int32, (levels, 128), 0)
    weights = jnp.zeros((levels, 128), F32)
    for k in range(levels):
        weights = jnp.where(level_of == k, w_ref[lev * levels + k], weights)
    weights = widen(weights, width)

    for side, row, interface, sign in (
        (0, 0, upper[0:1], -1.0),
        (1, rows - 1, lower[rows - 1 :], 1.0),
    ):
        tracer = first_send[side, 1]
        tracer_in = edge_row(1, side, True) + MOIST_CORRECTION * edge_row(2, side, True)
        flux_in = (
            spread(interface * 0.25)
            * (first_send[side, 0] + edge_row(0, side, True))
            * (tracer + tracer_in)
        )
        wind = wrapped(edge_row(3, side))
        around = wrapped(tracer)
        flux = 0.25 * (wind + east(wind)) * (around + east(around))
        change = (flux - west(flux, width))[:, :width]
        part = (
            tracer
            - spread(zonal[row : row + 1]) * change
            + sign * spread(merid[row : row + 1]) * flux_in
        )
        rest_send[side, 0] = edge_row(1, side)
        rest_send[side, 1] = edge_row(2, side)
        rest_send[side, 2] = part
        rows_send[side, 0:1] = jnp.sum(weights * part, axis=0, keepdims=True)
        rows_send[side, 1:2] = g_ref[row : row + 1, :]
    start_halos(1)
    start_halos(2)
    for load in loads[2:]:
        load.wait()

    def partial(k, carry):
        zonal_sum, merid_sum, own_sum = carry
        weight = w_ref[lev * levels + k]
        tracer = t_ref[k] + MOIST_CORRECTION * q_ref[k]
        around = wrapped(tracer)
        wind = wrapped(u_ref[k])
        zonal_sum += weight * ((wind + east(wind)) * (around + east(around)))
        cross = v_ref[k]
        merid_sum += weight * (
            (cross + pltpu.roll(cross, rows - 1, 0)) * (tracer + pltpu.roll(tracer, rows - 1, 0))
        )
        return zonal_sum, merid_sum, own_sum + weight * tracer

    zonal_sum, merid_sum, own_sum = lax.fori_loop(
        0,
        levels,
        partial,
        (jnp.zeros((rows, full), F32), jnp.zeros((rows, width), F32), jnp.zeros((rows, width), F32)),
        unroll=True,
    )
    north_sum = jnp.where(row_of < rows - 1, 0.25 * upper_wide * merid_sum, 0.0)
    slab_sum = (
        own_sum
        - zonal_wide * (0.25 * (zonal_sum - west(zonal_sum, width)))[:, :width]
        - merid_wide * (north_sum - pltpu.roll(north_sum, 1, 0))
    )

    sum_send[0] = slab_sum[:half]
    sum_send[1] = slab_sum[half:]

    def along(ssem, rsem, source, target, here, leg, other, slab):
        return pltpu.make_async_remote_copy(
            src_ref=source,
            dst_ref=target.at[here],
            send_sem=ssem.at[leg, other],
            recv_sem=rsem.at[leg, here],
            device_id=(lat, slab),
            device_id_type=MESH,
        )

    def to_y(leg, source, target, other):
        return along(y_ssem, y_rsem, source, target, y, leg, other, x * along_y + other)

    def to_x(leg, source, target, other):
        return along(x_ssem, x_rsem, source, target, x, leg, other, other * along_y + y)

    def wait_slot(target, slot, sem):
        pltpu.make_async_copy(target.at[slot], target.at[slot], sem).wait()

    def start(copy):
        copy.start()

    def wait_send(copy):
        copy.wait_send()

    steps = sorted(range(1, along_y), key=lambda step: -min(step, along_y - step))
    swapped = jnp.logical_not(first_band)

    def meet_along_y(part, act):
        for step in steps:
            other = (y + step) % along_y
            wanted = (x > 0) | ((other < y) & ((other > 0) | swapped))
            pl.when(wanted)(lambda other=other: act(to_y(part, sum_send.at[part], meet_y.at[part], other)))

    def meet_along_x(act):
        lax.fori_loop(0, x, lambda other, c: (act(to_x(2, sum_send.at[1], meet_x, other)), c)[1], 0)

    def far_along_x(part, act):
        begin = jnp.where(first_band & (y == 0), 1, 0)
        lax.fori_loop(
            begin, x, lambda other, c: (act(to_x(part, total_send.at[part], far_x.at[part], other)), c)[1], 0
        )

    def far_along_y(act):
        for step in steps:
            other = (y + step) % along_y
            act(to_y(2, pair_send.at[(y + step) // along_y], far_y, other))

    def to_first(act):
        @pl.when(first_band & (x == 0) & (y > 0))
        def _():
            for part in (0, 1):
                act(to_y(part, sum_send.at[part], meet_y.at[part], 0))

        @pl.when(first_band & (x > 0) & (y == 0))
        def _():
            for part in (0, 1):
                act(to_x(part, total_send.at[part], far_x.at[part], 0))

        pl.when(first_band & (lev > 0))(lambda: act(to_lower(0)))

    def to_lower(other):
        return pltpu.make_async_remote_copy(
            src_ref=late_send,
            dst_ref=late_recv.at[lev],
            send_sem=late_ssem.at[other],
            recv_sem=late_rsem.at[lev],
            device_id=(lat, other),
            device_id_type=MESH,
        )

    def late_to_lower(act):
        lax.fori_loop(
            first_band.astype(jnp.int32), lev, lambda other, c: (act(to_lower(other)), c)[1], 0
        )

    meet_along_y(0, start)
    pl.when(first_band)(lambda: meet_along_y(1, start))
    pl.when(swapped)(lambda: meet_along_x(start))

    @pl.when(lev > 0)
    def _():
        wait_halos(0)
        wait_halos(1)
        for side, interface in ((0, north_interface), (1, south_interface)):
            mine = 1 - side
            wind = spread(interface * 0.25) * (first_send[mine, 0] + first_recv[side, 0])
            flux = wind * (first_send[mine, 1] + first_recv[side, 1])
            late_send[side : side + 1] = jnp.sum(weights * flux, axis=0, keepdims=True)
            late_send[side + 2 : side + 3] = rows_recv[side, 0:1]
        late_to_lower(start)

    def second_along_x(part):
        below, total_y = jnp.zeros((half, width), F32), sum_send[part]
        for step in range(1, along_y):
            other = (y + step) % along_y
            comes = (x > 0) | (other > y)

            @pl.when(comes)
            def _(other=other):
                wait_slot(meet_y.at[part], other, y_rsem.at[part, other])

            came = jnp.where(comes, meet_y[part, other], 0.0)
            total_y += came
            below += jnp.where(other > y, came, 0.0)
        total_send[part] = total_y
        hold_ref[part] = below
        far_along_x(part, start)

    def second_along_y():
        def add(other, total):
            wait_slot(meet_x, other, x_rsem.at[2, other])
            return total + meet_x[other]

        below = lax.fori_loop(x + 1, levs // along_y, add, jnp.zeros((half, width), F32))
        hold_ref[1] = below
        pair_send[0] = below
        pair_send[1] = below + sum_send[1]
        far_along_y(start)

    second_along_x(0)
    pl.when(first_band)(lambda: second_along_x(1))
    pl.when(swapped)(second_along_y)

    @pl.when(first_band & (lev > 0))
    def _():
        pl.semaphore_wait(ready, 1)

    to_first(start)

    half_zonal = 0.5 * zonal_wide
    inner_upper = jnp.where(row_of < rows - 1, 0.25 * upper_wide, 0.0)

    def local(step, below):
        k = levels - 1 - step
        weight = w_ref[lev * levels + k]
        wind, cross = u_ref[k], v_ref[k]
        wind_full = wrapped(wind)
        wind_pair = 0.25 * (wind_full + east(wind_full))
        cross_pair = inner_upper * (cross + pltpu.roll(cross, rows - 1, 0))

        def moved(tracer):
            around = wrapped(tracer)
            flux = wind_pair * (around + east(around))
            change = (flux - west(flux, width))[:, :width]
            north = cross_pair * (tracer + pltpu.roll(tracer, rows - 1, 0))
            return tracer - zonal_wide * change - merid_wide * (north - pltpu.roll(north, 1, 0))

        heat, humid = moved(t_ref[k]), moved(q_ref[k])
        t_out[k] = heat
        q_out[k] = humid
        below = below + weight * (heat + MOIST_CORRECTION * humid)
        c_out[k] = below
        around = wrapped(below)
        u_out[k] = wind - half_zonal * (east(around) - west(around, width))[:, :width]
        north = jnp.where(row_of == rows - 1, 0.0, pltpu.roll(below, rows - 1, 0))
        south = jnp.where(row_of == 0, 0.0, pltpu.roll(below, 1, 0))
        v_out[k] = cross - 0.5 * MERID_RATE * (north - south)
        return below

    lax.fori_loop(0, levels, local, jnp.zeros((rows, width), F32), unroll=2)

    def from_below(value):
        reach = 1
        while reach < levels:
            lower_part = pltpu.roll(value, levels - reach, 0)
            value = value + jnp.where(level_wide + reach < levels, lower_part, 0.0)
            reach *= 2
        return value

    level_wide = lax.broadcasted_iota(jnp.int32, (levels, width), 0)
    pl.when(lev == 0)(lambda: (wait_halos(0), wait_halos(1), None)[-1])
    wait_halos(2)
    for side, exists, row, beside_row, interface, merid_edge, sign in (
        (0, has_north, rows - 1, rows - 2, north_interface, merid_north, 1.0),
        (1, has_south, 0, 1, south_interface, merid_south, -1.0),
    ):
        mine = 1 - side
        wind = spread(interface * 0.25) * (first_send[mine, 0] + first_recv[side, 0])
        heat_flux = wind * (rest_send[mine, 0] + rest_recv[side, 0])
        humid_flux = wind * (rest_send[mine, 1] + rest_recv[side, 1])
        out = sign * spread(merid[row : row + 1])
        t_out[:, row, :] = t_out[:, row, :] - out * heat_flux
        q_out[:, row, :] = q_out[:, row, :] - out * humid_flux
        flux = heat_flux + MOIST_CORRECTION * humid_flux
        edge = from_below(weights * out * flux)
        beyond = weights * (rest_recv[side, 2] + sign * spread(merid_edge) * flux)
        beyond = from_below(jnp.where(exists, beyond, 0.0))
        c_out[:, row, :] = c_out[:, row, :] - edge
        around = wrapped(edge)
        turn = (east(around) - west(around, width))[:, :width]
        u_out[:, row, :] = u_out[:, row, :] + 0.5 * spread(zonal[row : row + 1]) * turn
        across = 0.5 * MERID_RATE * sign
        v_out[:, row, :] = v_out[:, row, :] - across * beyond
        v_out[:, beside_row, :] = v_out[:, beside_row, :] + across * edge

    def last_along_x(part):
        def add(other, total):
            wait_slot(far_x.at[part], other, x_rsem.at[part, other])
            return total + far_x[part, other]

        hold_ref[part] = lax.fori_loop(x + 1, levs // along_y, add, hold_ref[part])

    def last_along_y():
        total = hold_ref[1]
        for step in range(1, along_y):
            other = (y + step) % along_y
            wait_slot(far_y, other, y_rsem.at[2, other])
            total += far_y[other]
        hold_ref[1] = total

    last_along_x(0)
    pl.when(first_band)(lambda: last_along_x(1))
    pl.when(swapped)(last_along_y)
    total = g_ref[...] + jnp.concatenate([hold_ref[0], hold_ref[1]], axis=0)

    around = wrapped(total)
    b_out[0] = total
    b_out[1] = half_zonal * (east(around) - west(around, width))[:, :width]
    north = jnp.where(row_of == rows - 1, 0.0, pltpu.roll(total, rows - 1, 0))
    south = jnp.where(row_of == 0, 0.0, pltpu.roll(total, 1, 0))
    b_out[2] = 0.5 * MERID_RATE * (north - south)

    def add_late(other, total):
        wait_slot(late_recv, other, late_rsem.at[other])
        return total + late_recv[other]

    edges = lax.fori_loop(lev + 1, levs, add_late, jnp.zeros(late_send.shape, F32))
    for side, exists, row, beside_row, merid_edge, sign in (
        (0, has_north, rows - 1, rows - 2, merid_north, 1.0),
        (1, has_south, 0, 1, merid_south, -1.0),
    ):
        flux = edges[side : side + 1]
        change = -sign * merid_wide[row : row + 1] * flux
        beyond = rows_recv[side, 1:2] + edges[side + 2 : side + 3] + sign * widen(merid_edge, width) * flux
        around = wrapped(change)
        turn = (east(around) - west(around, width))[:, :width]
        across = 0.5 * MERID_RATE * sign
        b_out[0, row : row + 1] += change
        b_out[1, row : row + 1] += half_zonal[row : row + 1] * turn
        b_out[2, row : row + 1] += across * jnp.where(exists, beyond, 0.0)
        b_out[2, beside_row : beside_row + 1] += across * change

    for kind in range(3):
        pl.when(has_south)(halos[kind][0].wait_send)
        pl.when(has_north)(halos[kind][1].wait_send)
    meet_along_y(0, wait_send)
    far_along_x(0, wait_send)

    @pl.when(first_band)
    def _():
        meet_along_y(1, wait_send)
        far_along_x(1, wait_send)

    @pl.when(swapped)
    def _():
        meet_along_x(wait_send)
        far_along_y(wait_send)

    to_first(wait_send)
    late_to_lower(wait_send)


def finish_kernel(t_in, q_in, u_in, v_in, c_in, b_in, t, q, u, v, h, u_new, v_new, h_new, sems):
    copies = [
        pltpu.make_async_copy(source, target, sems.at[n])
        for n, (source, target) in enumerate([(t_in, t), (q_in, q), (h_new, h), (u_new, u), (v_new, v)])
    ]
    copies[0].start()
    copies[1].start()
    for k in range(t_in.shape[0]):
        h_new[k] = c_in[k] + b_in[0]
    copies[2].start()
    for k in range(t_in.shape[0]):
        u_new[k] = u_in[k] - b_in[1]
    copies[3].start()
    for k in range(t_in.shape[0]):
        v_new[k] = v_in[k] - b_in[2]
    copies[4].start()
    for copy in copies:
        copy.wait()


def body(zonal, poleward, heat, humidity, ground, weights):
    levels, rows, width = heat.shape
    levs = lax.axis_size("lev")
    along_y = 4 if levs % 4 == 0 else levs
    along_x, half = levs // along_y, rows // 2
    slab = (levels, rows, width)
    anywhere = pl.BlockSpec(memory_space=pl.ANY)
    vmem = pl.BlockSpec(memory_space=pltpu.VMEM)
    dma = pltpu.SemaphoreType.DMA
    args = [pltpu.with_memory_space_constraint(x, pltpu.HBM) for x in (zonal, poleward, heat, humidity, ground, weights)]
    parts = pl.pallas_call(
        advect_kernel,
        name="advect",
        out_shape=[pltpu.VMEM(slab, F32)] * 5 + [pltpu.VMEM((3, rows, width), F32)],
        in_specs=[anywhere] * 6,
        out_specs=[vmem] * 6,
        scratch_shapes=[pltpu.VMEM(slab, F32)] * 4
        + [
            pltpu.VMEM((rows, width), F32),
            pltpu.SMEM(weights.shape, F32),
            pltpu.VMEM((4, 2, levels, 2, width), F32),
            pltpu.VMEM((2, 2, levels, width), F32),
            pltpu.VMEM((2, 2, levels, width), F32),
            pltpu.VMEM((2, 2, width), F32),
            pltpu.VMEM((2, 2, width), F32),
            pltpu.VMEM((2, 3, levels, width), F32),
            pltpu.VMEM((2, 3, levels, width), F32),
            pltpu.VMEM((2, half, width), F32),
            pltpu.VMEM((2, along_y, half, width), F32),
            pltpu.VMEM((2, half, width), F32),
            pltpu.VMEM((2, along_x, half, width), F32),
            pltpu.VMEM((along_x, half, width), F32),
            pltpu.VMEM((2, half, width), F32),
            pltpu.VMEM((along_y, half, width), F32),
            pltpu.VMEM((2, half, width), F32),
            pltpu.VMEM((4, width), F32),
            pltpu.VMEM((levs, 4, width), F32),
            dma((6,)),
            dma((4, 2)),
            dma((3, 2)),
            dma((3, 2)),
            dma((3, along_y)),
            dma((3, along_y)),
            dma((3, along_x)),
            dma((3, along_x)),
            dma((levs,)),
            dma((levs,)),
            pltpu.SemaphoreType.REGULAR,
        ],
        compiler_params=pltpu.CompilerParams(
            collective_id=0, has_side_effects=True, vmem_limit_bytes=32 * 2**20
        ),
    )(*args)
    return pl.pallas_call(
        finish_kernel,
        name="finish",
        out_shape=[jax.ShapeDtypeStruct(slab, F32)] * 5,
        in_specs=[vmem] * 6,
        out_specs=[anywhere] * 5,
        scratch_shapes=[pltpu.VMEM(slab, F32)] * 3 + [dma((5,))],
        compiler_params=pltpu.CompilerParams(vmem_limit_bytes=16 * 2**20),
    )(*parts)


def solution(mesh):
    slab = P("lev", "lat", None)
    return jax.shard_map(
        body,
        mesh=mesh,
        in_specs=(slab,) * 4 + (P("lat", None), P()),
        out_specs=(slab,) * 5,
        check_vma=False,
    )
```

```python
import functools
import jax
import jax.numpy as jnp
from jax import lax
from jax.experimental import pallas as pl
from jax.experimental.pallas import tpu as pltpu
from jax.sharding import PartitionSpec as P

ZONAL_RATE = 0.1
MERID_RATE = 0.25
POLAR_CAP = 0.2
MOIST_CORRECTION = 0.6
F32 = jnp.float32
MESH = pl.DeviceIdType.MESH


def lat_weights(row_index, circle_sum):
    spacing = jnp.pi / circle_sum
    middle_boxes = jnp.cos(-jnp.pi / 2 + (row_index + 0.5) * spacing)
    upper_interface = jnp.where(
        row_index + 1.0 < circle_sum, jnp.cos(-jnp.pi / 2 + (row_index + 1.0) * spacing), 0.0
    )
    lower_interface = jnp.where(row_index > 0.5, jnp.cos(-jnp.pi / 2 + row_index * spacing), 0.0)
    return middle_boxes, upper_interface, lower_interface


def widen(column, width):
    whole, rest = width // 128, width % 128
    parts = [column] * whole + ([column[:, :rest]] if rest else [])
    return jnp.concatenate(parts, axis=1)


def wrapped(value):
    width = value.shape[1]
    extra = -width % 128
    if extra == 0:
        return value
    return jnp.concatenate([value, value[:, :extra]], axis=1)


def east(full):
    return pltpu.roll(full, full.shape[1] - 1, 1)


def west(full, width):
    size = full.shape[1]
    rolled = pltpu.roll(full, 1, 1)
    if size == width:
        return rolled
    last = pltpu.roll(full[:, size - 128 :], 128 - (width - 1 - (size - 128)), 1)
    lane = lax.broadcasted_iota(jnp.int32, last.shape, 1)
    start = jnp.where(lane == 0, last, rolled[:, :128])
    return jnp.concatenate([start, rolled[:, 128:]], axis=1)


def advect_kernel(
    u_hbm, v_hbm, t_hbm, q_hbm, g_hbm, w_hbm,
    t_out, q_out, u_out, v_out, c_out, b_out,
    whole_ref, g_ref, w_ref, edge_rows,
    first_send, first_recv, rows_send, rows_recv, rest_send, rest_recv,
    sum_send, meet_y, total_send, far_x, meet_x, pair_send, far_y, hold_ref,
    late_send, late_recv,
    in_sem, halo_ssem, halo_rsem, sum_ssem, sum_rsem, late_ssem, late_rsem, ready,
):
    lat, lev = lax.axis_index("lat"), lax.axis_index("lev")
    lats, levs = lax.axis_size("lat"), lax.axis_size("lev")
    along_y = meet_y.shape[1]
    groups = levs // along_y
    x, y = lev // along_y, lev % along_y
    v_ref, t_ref, q_ref, u_ref = [whole_ref.at[kind] for kind in range(4)]
    levels, rows, width = t_ref.shape
    half = rows // 2
    circle_sum = rows * lats
    full = width + (-width % 128)
    has_south, has_north = lat > 0, lat < lats - 1

    barrier = pltpu.get_barrier_semaphore()
    first_band = lat == 0
    first = first_band & (lev == 0)

    def greet(band, slab):
        pl.semaphore_signal(barrier, inc=1, device_id=(band, slab), device_id_type=MESH)

    @pl.when(has_south)
    def _():
        greet(lat - 1, lev)

    @pl.when(has_north)
    def _():
        greet(lat + 1, lev)

    pl.when(first_band & (lev > 0))(lambda: greet(lat, 0))

    @pl.when(jnp.logical_not(first))
    def _():
        lax.fori_loop(lev + 1, levs, lambda slab, c: (greet(lat, slab), c)[1], 0)
        known = jnp.maximum(x * along_y, first_band.astype(jnp.int32))
        lax.fori_loop(known, lev, lambda slab, c: (greet(lat, slab), c)[1], 0)

    edge_loads = [
        pltpu.make_async_copy(
            source.at[:, pl.ds(side * (rows - 2), 2), :], edge_rows.at[kind, side], in_sem.at[2]
        )
        for kind, source in enumerate([v_hbm, t_hbm, q_hbm, u_hbm])
        for side in (0, 1)
    ]
    small_loads = [
        pltpu.make_async_copy(w_hbm, w_ref, in_sem.at[0]),
        pltpu.make_async_copy(g_hbm, g_ref, in_sem.at[1]),
    ]
    whole_loads = [
        pltpu.make_async_copy(source, whole_ref.at[kind], in_sem.at[3])
        for kind, source in enumerate([v_hbm, t_hbm, q_hbm, u_hbm])
    ]
    for load in edge_loads + small_loads:
        load.start()

    band = (lat * rows + lax.broadcasted_iota(jnp.int32, (rows, 128), 0)).astype(F32)
    centre, upper, lower = lat_weights(band, circle_sum)
    zonal = ZONAL_RATE / jnp.maximum(centre, POLAR_CAP)
    merid = MERID_RATE / centre
    beside = lat * rows - 1 + (rows + 1) * lax.broadcasted_iota(jnp.int32, (8, 128), 0)
    beside_centre, _, _ = lat_weights(beside.astype(F32), circle_sum)
    merid_beside = MERID_RATE / beside_centre
    south_interface, north_interface = lower[0:1], upper[rows - 1 :]
    merid_south, merid_north = merid_beside[0:1], merid_beside[1:2]
    row_of = lax.broadcasted_iota(jnp.int32, (rows, width), 0)
    upper_wide = widen(upper, width)
    zonal_wide, merid_wide = widen(zonal, width), widen(merid, width)

    def spread(row):
        return widen(jnp.broadcast_to(row, (levels, 128)), width)

    for side, exists in ((0, has_north), (1, has_south)):

        @pl.when(jnp.logical_not(exists))
        def _(side=side):
            first_recv[side] = jnp.zeros(first_recv.shape[1:], F32)
            rows_recv[side] = jnp.zeros(rows_recv.shape[1:], F32)
            rest_recv[side] = jnp.zeros(rest_recv.shape[1:], F32)

    def halo(kind, send, recv, side):
        return pltpu.make_async_remote_copy(
            src_ref=send.at[side],
            dst_ref=recv.at[side],
            send_sem=halo_ssem.at[kind, side],
            recv_sem=halo_rsem.at[kind, side],
            device_id=(lat - 1 if side == 0 else lat + 1, lev),
            device_id_type=MESH,
        )

    halos = [
        [halo(kind, send, recv, side) for side in (0, 1)]
        for kind, (send, recv) in enumerate(
            [(first_send, first_recv), (rows_send, rows_recv), (rest_send, rest_recv)]
        )
    ]

    def start_halos(kind):
        pl.when(has_south)(halos[kind][0].start)
        pl.when(has_north)(halos[kind][1].start)

    def wait_halos(kind):
        pl.when(has_south)(halos[kind][1].wait_recv)
        pl.when(has_north)(halos[kind][0].wait_recv)

    pltpu.make_async_copy(edge_rows, edge_rows, in_sem.at[2]).wait()
    for load in whole_loads:
        load.start()

    def edge_row(kind, side, inner=False):
        return edge_rows[kind, side, :, side if not inner else 1 - side, :]

    for side in (0, 1):
        first_send[side, 0] = edge_row(0, side)
        first_send[side, 1] = edge_row(1, side) + MOIST_CORRECTION * edge_row(2, side)
    def enter():
        pl.semaphore_wait(
            barrier,
            jnp.where(first, levs - 1, lev - first_band.astype(jnp.int32) + along_y - 1 - y)
            + has_south.astype(jnp.int32)
            + has_north.astype(jnp.int32),
        )
        start_halos(0)

    ahead = lat % 2 == 1
    pl.when(jnp.logical_not(ahead))(enter)
    for load in small_loads:
        load.wait()
    level_of = lax.broadcasted_iota(jnp.int32, (levels, 128), 0)
    weights = jnp.zeros((levels, 128), F32)
    for k in range(levels):
        weights = jnp.where(level_of == k, w_ref[lev * levels + k], weights)
    weights = widen(weights, width)

    for side, row, interface, sign in (
        (0, 0, upper[0:1], -1.0),
        (1, rows - 1, lower[rows - 1 :], 1.0),
    ):
        tracer = first_send[side, 1]
        tracer_in = edge_row(1, side, True) + MOIST_CORRECTION * edge_row(2, side, True)
        flux_in = (
            spread(interface * 0.25)
            * (first_send[side, 0] + edge_row(0, side, True))
            * (tracer + tracer_in)
        )
        wind = wrapped(edge_row(3, side))
        around = wrapped(tracer)
        flux = 0.25 * (wind + east(wind)) * (around + east(around))
        change = (flux - west(flux, width))[:, :width]
        part = (
            tracer
            - spread(zonal[row : row + 1]) * change
            + sign * spread(merid[row : row + 1]) * flux_in
        )
        rest_send[side, 0] = edge_row(1, side)
        rest_send[side, 1] = edge_row(2, side)
        rest_send[side, 2] = part
        rows_send[side, 0:1] = jnp.sum(weights * part, axis=0, keepdims=True)
        rows_send[side, 1:2] = g_ref[row : row + 1, :]

    def start_rest():
        start_halos(1)
        start_halos(2)

        @pl.when(first)
        def _():
            def answer(slab, carry):
                pl.semaphore_signal(ready, inc=1, device_id=(lat, slab), device_id_type=MESH)
                return carry

            lax.fori_loop(1, levs, answer, 0)

    pl.when(jnp.logical_not(ahead))(start_rest)
    pltpu.make_async_copy(whole_ref, whole_ref, in_sem.at[3]).wait()

    def partial(k, carry):
        zonal_sum, merid_sum, own_sum = carry
        weight = w_ref[lev * levels + k]
        tracer = t_ref[k] + MOIST_CORRECTION * q_ref[k]
        around = wrapped(tracer)
        wind = wrapped(u_ref[k])
        zonal_sum += weight * ((wind + east(wind)) * (around + east(around)))
        cross = v_ref[k]
        merid_sum += weight * (
            (cross + pltpu.roll(cross, rows - 1, 0)) * (tracer + pltpu.roll(tracer, rows - 1, 0))
        )
        return zonal_sum, merid_sum, own_sum + weight * tracer

    zonal_sum, merid_sum, own_sum = lax.fori_loop(
        0,
        levels,
        partial,
        (jnp.zeros((rows, full), F32), jnp.zeros((rows, width), F32), jnp.zeros((rows, width), F32)),
        unroll=True,
    )
    north_sum = jnp.where(row_of < rows - 1, 0.25 * upper_wide * merid_sum, 0.0)
    slab_sum = (
        own_sum
        - zonal_wide * (0.25 * (zonal_sum - west(zonal_sum, width)))[:, :width]
        - merid_wide * (north_sum - pltpu.roll(north_sum, 1, 0))
    )

    sum_send[0] = slab_sum[:half]
    sum_send[1] = slab_sum[half:]

    def along(source, target, here, leg, part, slab):
        return pltpu.make_async_remote_copy(
            src_ref=source,
            dst_ref=target.at[here],
            send_sem=sum_ssem.at[leg, part],
            recv_sem=sum_rsem.at[leg, part],
            device_id=(lat, slab),
            device_id_type=MESH,
        )

    def to_y(leg, part, source, target, other):
        return along(source, target, y, leg, part, x * along_y + other)

    def to_x(leg, part, source, target, other):
        return along(source, target, x, leg, part, other * along_y + y)

    def wait_blocks(count, blocks, sem):
        for some in range(1, blocks.shape[0]):

            @pl.when(count == some)
            def _(some=some):
                taken = blocks.at[pl.ds(0, some)]
                pltpu.make_async_copy(taken, taken, sem).wait()

    def start(copy):
        copy.start()

    steps = sorted(range(1, along_y), key=lambda step: -min(step, along_y - step))
    swapped = jnp.logical_not(first_band)
    turned = (ahead, swapped)

    def meet_along_y(part, act):
        for step in steps:
            other = (y + step) % along_y
            wanted = (x > 0) | ((other < y) & ((other > 0) | swapped))
            pl.when(wanted)(lambda other=other: act(to_y(0, part, sum_send.at[part], meet_y.at[part], other)))

    def meet_along_x(part, act):
        lax.fori_loop(
            0, x, lambda other, c: (act(to_x(0, part, sum_send.at[part], meet_x.at[part], other)), c)[1], 0
        )

    def far_along_x(part, act):
        begin = jnp.where(first_band & (y == 0), 1, 0)
        lax.fori_loop(
            begin, x, lambda other, c: (act(to_x(1, part, total_send.at[part], far_x.at[part], other)), c)[1], 0
        )

    def far_along_y(part, act):
        for step in steps:
            other = (y + step) % along_y
            act(to_y(1, part, pair_send.at[part, (y + step) // along_y], far_y.at[part], other))

    def to_first(act):
        @pl.when(first_band & (x == 0) & (y > 0))
        def _():
            for part in (0, 1):
                act(to_y(0, part, sum_send.at[part], meet_y.at[part], 0))

        @pl.when(first_band & (x > 0) & (y == 0))
        def _():
            for part in (0, 1):
                act(to_x(1, part, total_send.at[part], far_x.at[part], 0))

        pl.when(first_band & (lev > 0))(lambda: act(to_lower(0)))

    def to_lower(other):
        return pltpu.make_async_remote_copy(
            src_ref=late_send,
            dst_ref=late_recv.at[lev],
            send_sem=late_ssem.at[0],
            recv_sem=late_rsem.at[0],
            device_id=(lat, other),
            device_id_type=MESH,
        )

    def late_to_lower(act):
        lax.fori_loop(
            first_band.astype(jnp.int32), lev, lambda other, c: (act(to_lower(other)), c)[1], 0
        )

    pl.when(ahead)(lambda: (enter(), start_rest(), None)[-1])
    for part in (0, 1):
        pl.when(jnp.logical_not(turned[part]))(lambda part=part: meet_along_y(part, start))
        pl.when(turned[part])(lambda part=part: meet_along_x(part, start))

    @pl.when(lev > 0)
    def _():
        wait_halos(0)
        wait_halos(1)
        for side, interface in ((0, north_interface), (1, south_interface)):
            mine = 1 - side
            wind = spread(interface * 0.25) * (first_send[mine, 0] + first_recv[side, 0])
            flux = wind * (first_send[mine, 1] + first_recv[side, 1])
            late_send[side : side + 1] = jnp.sum(weights * flux, axis=0, keepdims=True)
            late_send[side + 2 : side + 3] = rows_recv[side, 0:1]
        late_to_lower(start)

    def second_along_x(part):
        wait_blocks(jnp.where(x > 0, along_y - 1, along_y - 1 - y), meet_y.at[part], sum_rsem.at[0, part])
        below, total_y = jnp.zeros((half, width), F32), sum_send[part]
        for step in range(1, along_y):
            other = (y + step) % along_y
            comes = (x > 0) | (other > y)
            came = jnp.where(comes, meet_y[part, other], 0.0)
            total_y += came
            below += jnp.where(other > y, came, 0.0)
        total_send[part] = total_y
        hold_ref[part] = below
        far_along_x(part, start)

    def second_along_y(part):
        wait_blocks(groups - 1 - x, meet_x.at[part], sum_rsem.at[0, part])

        def add(other, total):
            return total + meet_x[part, other]

        below = lax.fori_loop(x + 1, levs // along_y, add, jnp.zeros((half, width), F32))
        hold_ref[part] = below
        pair_send[part, 0] = below
        pair_send[part, 1] = below + sum_send[part]
        far_along_y(part, start)

    for part in (0, 1):
        pl.when(jnp.logical_not(turned[part]))(lambda part=part: second_along_x(part))
        pl.when(turned[part])(lambda part=part: second_along_y(part))

    @pl.when(first_band & (lev > 0))
    def _():
        pl.semaphore_wait(ready, 1)

    to_first(start)

    half_zonal = 0.5 * zonal_wide
    inner_upper = jnp.where(row_of < rows - 1, 0.25 * upper_wide, 0.0)

    def local(step, below):
        k = levels - 1 - step
        weight = w_ref[lev * levels + k]
        wind, cross = u_ref[k], v_ref[k]
        wind_full = wrapped(wind)
        wind_pair = 0.25 * (wind_full + east(wind_full))
        cross_pair = inner_upper * (cross + pltpu.roll(cross, rows - 1, 0))

        def moved(tracer):
            around = wrapped(tracer)
            flux = wind_pair * (around + east(around))
            change = (flux - west(flux, width))[:, :width]
            north = cross_pair * (tracer + pltpu.roll(tracer, rows - 1, 0))
            return tracer - zonal_wide * change - merid_wide * (north - pltpu.roll(north, 1, 0))

        heat, humid = moved(t_ref[k]), moved(q_ref[k])
        t_out[k] = heat
        q_out[k] = humid
        below = below + weight * (heat + MOIST_CORRECTION * humid)
        c_out[k] = below
        around = wrapped(below)
        u_out[k] = wind - half_zonal * (east(around) - west(around, width))[:, :width]
        north = jnp.where(row_of == rows - 1, 0.0, pltpu.roll(below, rows - 1, 0))
        south = jnp.where(row_of == 0, 0.0, pltpu.roll(below, 1, 0))
        v_out[k] = cross - 0.5 * MERID_RATE * (north - south)
        return below

    lax.fori_loop(0, levels, local, jnp.zeros((rows, width), F32), unroll=2)

    def from_below(value):
        reach = 1
        while reach < levels:
            lower_part = pltpu.roll(value, levels - reach, 0)
            value = value + jnp.where(level_wide + reach < levels, lower_part, 0.0)
            reach *= 2
        return value

    level_wide = lax.broadcasted_iota(jnp.int32, (levels, width), 0)
    pl.when(lev == 0)(lambda: (wait_halos(0), wait_halos(1), None)[-1])
    wait_halos(2)
    for side, exists, row, beside_row, interface, merid_edge, sign in (
        (0, has_north, rows - 1, rows - 2, north_interface, merid_north, 1.0),
        (1, has_south, 0, 1, south_interface, merid_south, -1.0),
    ):
        mine = 1 - side
        wind = spread(interface * 0.25) * (first_send[mine, 0] + first_recv[side, 0])
        heat_flux = wind * (rest_send[mine, 0] + rest_recv[side, 0])
        humid_flux = wind * (rest_send[mine, 1] + rest_recv[side, 1])
        out = sign * spread(merid[row : row + 1])
        t_out[:, row, :] = t_out[:, row, :] - out * heat_flux
        q_out[:, row, :] = q_out[:, row, :] - out * humid_flux
        flux = heat_flux + MOIST_CORRECTION * humid_flux
        edge = from_below(weights * out * flux)
        beyond = weights * (rest_recv[side, 2] + sign * spread(merid_edge) * flux)
        beyond = from_below(jnp.where(exists, beyond, 0.0))
        c_out[:, row, :] = c_out[:, row, :] - edge
        around = wrapped(edge)
        turn = (east(around) - west(around, width))[:, :width]
        u_out[:, row, :] = u_out[:, row, :] + 0.5 * spread(zonal[row : row + 1]) * turn
        across = 0.5 * MERID_RATE * sign
        v_out[:, row, :] = v_out[:, row, :] - across * beyond
        v_out[:, beside_row, :] = v_out[:, beside_row, :] + across * edge

    def last_along_x(part):
        wait_blocks(groups - 1 - x, far_x.at[part], sum_rsem.at[1, part])

        def add(other, total):
            return total + far_x[part, other]

        hold_ref[part] = lax.fori_loop(x + 1, levs // along_y, add, hold_ref[part])

    def last_along_y(part):
        wait_blocks(along_y - 1, far_y.at[part], sum_rsem.at[1, part])
        total = hold_ref[part]
        for step in range(1, along_y):
            other = (y + step) % along_y
            total += far_y[part, other]
        hold_ref[part] = total

    for part in (0, 1):
        pl.when(jnp.logical_not(turned[part]))(lambda part=part: last_along_x(part))
        pl.when(turned[part])(lambda part=part: last_along_y(part))
    total = g_ref[...] + jnp.concatenate([hold_ref[0], hold_ref[1]], axis=0)

    around = wrapped(total)
    b_out[0] = total
    b_out[1] = half_zonal * (east(around) - west(around, width))[:, :width]
    north = jnp.where(row_of == rows - 1, 0.0, pltpu.roll(total, rows - 1, 0))
    south = jnp.where(row_of == 0, 0.0, pltpu.roll(total, 1, 0))
    b_out[2] = 0.5 * MERID_RATE * (north - south)

    def add_late(other, total):
        return total + late_recv[other]

    wait_blocks(levs - 1 - lev, late_recv, late_rsem.at[0])
    edges = lax.fori_loop(lev + 1, levs, add_late, jnp.zeros(late_send.shape, F32))
    for side, exists, row, beside_row, merid_edge, sign in (
        (0, has_north, rows - 1, rows - 2, merid_north, 1.0),
        (1, has_south, 0, 1, merid_south, -1.0),
    ):
        flux = edges[side : side + 1]
        change = -sign * merid_wide[row : row + 1] * flux
        beyond = rows_recv[side, 1:2] + edges[side + 2 : side + 3] + sign * widen(merid_edge, width) * flux
        around = wrapped(change)
        turn = (east(around) - west(around, width))[:, :width]
        across = 0.5 * MERID_RATE * sign
        b_out[0, row : row + 1] += change
        b_out[1, row : row + 1] += half_zonal[row : row + 1] * turn
        b_out[2, row : row + 1] += across * jnp.where(exists, beyond, 0.0)
        b_out[2, beside_row : beside_row + 1] += across * change

    for kind in range(3):
        pl.when(has_south)(halos[kind][0].wait_send)
        pl.when(has_north)(halos[kind][1].wait_send)

    for part in (0, 1):

        @pl.when(jnp.logical_not(turned[part]))
        def _(part=part):
            wait_blocks(jnp.where(x > 0, along_y - 1, y), meet_y.at[part], sum_ssem.at[0, part])
            wait_blocks(x, far_x.at[part], sum_ssem.at[1, part])

        @pl.when(turned[part])
        def _(part=part):
            wait_blocks(x, meet_x.at[part], sum_ssem.at[0, part])
            wait_blocks(along_y - 1, far_y.at[part], sum_ssem.at[1, part])

    wait_blocks(lev, late_recv, late_ssem.at[0])


def finish_kernel(t_in, q_in, u_in, v_in, c_in, b_in, t, q, u, v, h, u_new, v_new, h_new, sems):
    copies = [
        pltpu.make_async_copy(source, target, sems.at[n])
        for n, (source, target) in enumerate([(t_in, t), (q_in, q), (h_new, h), (u_new, u), (v_new, v)])
    ]
    copies[0].start()
    copies[1].start()
    for k in range(t_in.shape[0]):
        h_new[k] = c_in[k] + b_in[0]
    copies[2].start()
    for k in range(t_in.shape[0]):
        u_new[k] = u_in[k] - b_in[1]
    copies[3].start()
    for k in range(t_in.shape[0]):
        v_new[k] = v_in[k] - b_in[2]
    copies[4].start()
    for copy in copies:
        copy.wait()


def body(zonal, poleward, heat, humidity, ground, weights):
    levels, rows, width = heat.shape
    levs = lax.axis_size("lev")
    along_y = 4 if levs % 4 == 0 else levs
    along_x, half = levs // along_y, rows // 2
    slab = (levels, rows, width)
    anywhere = pl.BlockSpec(memory_space=pl.ANY)
    vmem = pl.BlockSpec(memory_space=pltpu.VMEM)
    dma = pltpu.SemaphoreType.DMA
    args = [pltpu.with_memory_space_constraint(x, pltpu.HBM) for x in (zonal, poleward, heat, humidity, ground, weights)]
    parts = pl.pallas_call(
        advect_kernel,
        name="advect",
        out_shape=[pltpu.VMEM(slab, F32)] * 5 + [pltpu.VMEM((3, rows, width), F32)],
        in_specs=[anywhere] * 6,
        out_specs=[vmem] * 6,
        scratch_shapes=[
            pltpu.VMEM((4,) + slab, F32),
            pltpu.VMEM((rows, width), F32),
            pltpu.SMEM(weights.shape, F32),
            pltpu.VMEM((4, 2, levels, 2, width), F32),
            pltpu.VMEM((2, 2, levels, width), F32),
            pltpu.VMEM((2, 2, levels, width), F32),
            pltpu.VMEM((2, 2, width), F32),
            pltpu.VMEM((2, 2, width), F32),
            pltpu.VMEM((2, 3, levels, width), F32),
            pltpu.VMEM((2, 3, levels, width), F32),
            pltpu.VMEM((2, half, width), F32),
            pltpu.VMEM((2, along_y, half, width), F32),
            pltpu.VMEM((2, half, width), F32),
            pltpu.VMEM((2, along_x, half, width), F32),
            pltpu.VMEM((2, along_x, half, width), F32),
            pltpu.VMEM((2, 2, half, width), F32),
            pltpu.VMEM((2, along_y, half, width), F32),
            pltpu.VMEM((2, half, width), F32),
            pltpu.VMEM((4, width), F32),
            pltpu.VMEM((levs, 4, width), F32),
            dma((4,)),
            dma((3, 2)),
            dma((3, 2)),
            dma((2, 2)),
            dma((2, 2)),
            dma((1,)),
            dma((1,)),
            pltpu.SemaphoreType.REGULAR,
        ],
        compiler_params=pltpu.CompilerParams(
            collective_id=0, has_side_effects=True, vmem_limit_bytes=32 * 2**20
        ),
    )(*args)
    return pl.pallas_call(
        finish_kernel,
        name="finish",
        out_shape=[jax.ShapeDtypeStruct(slab, F32)] * 5,
        in_specs=[vmem] * 6,
        out_specs=[anywhere] * 5,
        scratch_shapes=[pltpu.VMEM(slab, F32)] * 3 + [dma((5,))],
        compiler_params=pltpu.CompilerParams(vmem_limit_bytes=16 * 2**20),
    )(*parts)


def solution(mesh):
    slab = P("lev", "lat", None)
    return jax.shard_map(
        body,
        mesh=mesh,
        in_specs=(slab,) * 4 + (P("lat", None), P()),
        out_specs=(slab,) * 5,
        check_vma=False,
    )
```

```python
import functools
import jax
import jax.numpy as jnp
from jax import lax
from jax.experimental import pallas as pl
from jax.experimental.pallas import tpu as pltpu
from jax.sharding import PartitionSpec as P

ZONAL_RATE = 0.1
MERID_RATE = 0.25
POLAR_CAP = 0.2
MOIST_CORRECTION = 0.6
F32 = jnp.float32
MESH = pl.DeviceIdType.MESH


def lat_weights(row_index, circle_sum):
    spacing = jnp.pi / circle_sum
    middle_boxes = jnp.cos(-jnp.pi / 2 + (row_index + 0.5) * spacing)
    upper_interface = jnp.where(
        row_index + 1.0 < circle_sum, jnp.cos(-jnp.pi / 2 + (row_index + 1.0) * spacing), 0.0
    )
    lower_interface = jnp.where(row_index > 0.5, jnp.cos(-jnp.pi / 2 + row_index * spacing), 0.0)
    return middle_boxes, upper_interface, lower_interface


def widen(column, width):
    whole, rest = width // 128, width % 128
    parts = [column] * whole + ([column[:, :rest]] if rest else [])
    return jnp.concatenate(parts, axis=1)


def wrapped(value):
    width = value.shape[1]
    extra = -width % 128
    if extra == 0:
        return value
    return jnp.concatenate([value, value[:, :extra]], axis=1)


def east(full):
    return pltpu.roll(full, full.shape[1] - 1, 1)


def west(full, width):
    size = full.shape[1]
    rolled = pltpu.roll(full, 1, 1)
    if size == width:
        return rolled
    last = pltpu.roll(full[:, size - 128 :], 128 - (width - 1 - (size - 128)), 1)
    lane = lax.broadcasted_iota(jnp.int32, last.shape, 1)
    start = jnp.where(lane == 0, last, rolled[:, :128])
    return jnp.concatenate([start, rolled[:, 128:]], axis=1)


def advect_kernel(
    u_hbm, v_hbm, t_hbm, q_hbm, g_hbm, w_hbm,
    t_out, q_out, u_out, v_out, c_out, b_out,
    whole_ref, g_ref, w_ref, edge_rows,
    first_send, first_recv, rows_send, rows_recv, rest_send, rest_recv,
    sum_send, meet_y, total_send, far_x, meet_x, pair_send, far_y, hold_ref,
    late_send, late_recv,
    in_sem, halo_ssem, halo_rsem, sum_ssem, sum_rsem, late_ssem, late_rsem, ready,
):
    lat, lev = lax.axis_index("lat"), lax.axis_index("lev")
    lats, levs = lax.axis_size("lat"), lax.axis_size("lev")
    along_y = meet_y.shape[1]
    groups = levs // along_y
    x, y = lev // along_y, lev % along_y
    v_ref, t_ref, q_ref, u_ref = [whole_ref.at[kind] for kind in range(4)]
    levels, rows, width = t_ref.shape
    half = rows // 2
    circle_sum = rows * lats
    full = width + (-width % 128)
    has_south, has_north = lat > 0, lat < lats - 1

    barrier = pltpu.get_barrier_semaphore()
    first_band = lat == 0
    first = first_band & (lev == 0)

    def greet(band, slab):
        pl.semaphore_signal(barrier, inc=1, device_id=(band, slab), device_id_type=MESH)

    @pl.when(has_south)
    def _():
        greet(lat - 1, lev)

    @pl.when(has_north)
    def _():
        greet(lat + 1, lev)

    pl.when(first_band & (lev > 0))(lambda: greet(lat, 0))

    @pl.when(jnp.logical_not(first))
    def _():
        lax.fori_loop(lev + 1, levs, lambda slab, c: (greet(lat, slab), c)[1], 0)
        known = jnp.maximum(x * along_y, first_band.astype(jnp.int32))
        lax.fori_loop(known, lev, lambda slab, c: (greet(lat, slab), c)[1], 0)

    edge_loads = [
        pltpu.make_async_copy(
            source.at[:, pl.ds(side * (rows - 2), 2), :], edge_rows.at[kind, side], in_sem.at[2]
        )
        for kind, source in enumerate([v_hbm, t_hbm, q_hbm, u_hbm])
        for side in (0, 1)
    ]
    small_loads = [
        pltpu.make_async_copy(w_hbm, w_ref, in_sem.at[0]),
        pltpu.make_async_copy(g_hbm, g_ref, in_sem.at[1]),
    ]
    whole_loads = [
        pltpu.make_async_copy(source, whole_ref.at[kind], in_sem.at[3])
        for kind, source in enumerate([v_hbm, t_hbm, q_hbm, u_hbm])
    ]
    for load in edge_loads + small_loads + whole_loads:
        load.start()

    band = (lat * rows + lax.broadcasted_iota(jnp.int32, (rows, 128), 0)).astype(F32)
    centre, upper, lower = lat_weights(band, circle_sum)
    zonal = ZONAL_RATE / jnp.maximum(centre, POLAR_CAP)
    merid = MERID_RATE / centre
    beside = lat * rows - 1 + (rows + 1) * lax.broadcasted_iota(jnp.int32, (8, 128), 0)
    beside_centre, _, _ = lat_weights(beside.astype(F32), circle_sum)
    merid_beside = MERID_RATE / beside_centre
    south_interface, north_interface = lower[0:1], upper[rows - 1 :]
    merid_south, merid_north = merid_beside[0:1], merid_beside[1:2]
    row_of = lax.broadcasted_iota(jnp.int32, (rows, width), 0)
    upper_wide = widen(upper, width)
    zonal_wide, merid_wide = widen(zonal, width), widen(merid, width)

    def spread(row):
        return widen(jnp.broadcast_to(row, (levels, 128)), width)

    def clear(slab, carry):
        late_recv[slab] = jnp.zeros(late_recv.shape[1:], F32)
        return carry

    lax.fori_loop(0, lev + 1, clear, 0)

    for side, exists in ((0, has_north), (1, has_south)):

        @pl.when(jnp.logical_not(exists))
        def _(side=side):
            first_recv[side] = jnp.zeros(first_recv.shape[1:], F32)
            rows_recv[side] = jnp.zeros(rows_recv.shape[1:], F32)
            rest_recv[side] = jnp.zeros(rest_recv.shape[1:], F32)

    def halo(kind, send, recv, side):
        return pltpu.make_async_remote_copy(
            src_ref=send.at[side],
            dst_ref=recv.at[side],
            send_sem=halo_ssem.at[kind],
            recv_sem=halo_rsem.at[kind, side],
            device_id=(lat - 1 if side == 0 else lat + 1, lev),
            device_id_type=MESH,
        )

    halos = [
        [halo(kind, send, recv, side) for side in (0, 1)]
        for kind, (send, recv) in enumerate(
            [(first_send, first_recv), (rows_send, rows_recv), (rest_send, rest_recv)]
        )
    ]

    def start_halos(kind):
        pl.when(has_south)(halos[kind][0].start)
        pl.when(has_north)(halos[kind][1].start)

    def wait_halos(kind, side):
        pl.when(has_south if side == 1 else has_north)(halos[kind][side].wait_recv)

    pltpu.make_async_copy(edge_rows, edge_rows, in_sem.at[2]).wait()

    def edge_row(kind, side, inner=False):
        return edge_rows[kind, side, :, side if not inner else 1 - side, :]

    for side in (0, 1):
        first_send[side, 0] = edge_row(0, side)
        first_send[side, 1] = edge_row(1, side) + MOIST_CORRECTION * edge_row(2, side)
    def enter():
        pl.semaphore_wait(
            barrier,
            jnp.where(first, levs - 1, lev - first_band.astype(jnp.int32) + along_y - 1 - y)
            + has_south.astype(jnp.int32)
            + has_north.astype(jnp.int32),
        )
        start_halos(0)

    ahead = lat % 2 == 1
    pl.when(jnp.logical_not(ahead))(enter)
    for load in small_loads:
        load.wait()
    level_of = lax.broadcasted_iota(jnp.int32, (levels, 128), 0)
    weights = jnp.zeros((levels, 128), F32)
    for k in range(levels):
        weights = jnp.where(level_of == k, w_ref[lev * levels + k], weights)
    weights = widen(weights, width)

    for side, row, interface, sign in (
        (0, 0, upper[0:1], -1.0),
        (1, rows - 1, lower[rows - 1 :], 1.0),
    ):
        tracer = first_send[side, 1]
        tracer_in = edge_row(1, side, True) + MOIST_CORRECTION * edge_row(2, side, True)
        flux_in = (
            spread(interface * 0.25)
            * (first_send[side, 0] + edge_row(0, side, True))
            * (tracer + tracer_in)
        )
        wind = wrapped(edge_row(3, side))
        around = wrapped(tracer)
        flux = 0.25 * (wind + east(wind)) * (around + east(around))
        change = (flux - west(flux, width))[:, :width]
        part = (
            tracer
            - spread(zonal[row : row + 1]) * change
            + sign * spread(merid[row : row + 1]) * flux_in
        )
        rest_send[side, 0] = edge_row(1, side)
        rest_send[side, 1] = edge_row(2, side)
        rest_send[side, 2] = part
        rows_send[side, 0:1] = jnp.sum(weights * part, axis=0, keepdims=True)
        rows_send[side, 1:2] = g_ref[row : row + 1, :]

    def start_rest():
        start_halos(1)
        start_halos(2)

        @pl.when(first)
        def _():
            def answer(slab, carry):
                pl.semaphore_signal(ready, inc=1, device_id=(lat, slab), device_id_type=MESH)
                return carry

            lax.fori_loop(1, levs, answer, 0)

    pl.when(jnp.logical_not(ahead))(start_rest)
    pltpu.make_async_copy(whole_ref, whole_ref, in_sem.at[3]).wait()

    def partial(k, carry):
        zonal_sum, merid_sum, own_sum = carry
        weight = w_ref[lev * levels + k]
        tracer = t_ref[k] + MOIST_CORRECTION * q_ref[k]
        around = wrapped(tracer)
        wind = wrapped(u_ref[k])
        zonal_sum += weight * ((wind + east(wind)) * (around + east(around)))
        cross = v_ref[k]
        merid_sum += weight * (
            (cross + pltpu.roll(cross, rows - 1, 0)) * (tracer + pltpu.roll(tracer, rows - 1, 0))
        )
        return zonal_sum, merid_sum, own_sum + weight * tracer

    zonal_sum, merid_sum, own_sum = lax.fori_loop(
        0,
        levels,
        partial,
        (jnp.zeros((rows, full), F32), jnp.zeros((rows, width), F32), jnp.zeros((rows, width), F32)),
        unroll=True,
    )
    north_sum = jnp.where(row_of < rows - 1, 0.25 * upper_wide * merid_sum, 0.0)
    slab_sum = (
        own_sum
        - zonal_wide * (0.25 * (zonal_sum - west(zonal_sum, width)))[:, :width]
        - merid_wide * (north_sum - pltpu.roll(north_sum, 1, 0))
    )

    sum_send[0] = slab_sum[:half]
    sum_send[1] = slab_sum[half:]

    def along(source, target, here, leg, part, slab):
        return pltpu.make_async_remote_copy(
            src_ref=source,
            dst_ref=target.at[here],
            send_sem=sum_ssem.at[leg, part],
            recv_sem=sum_rsem.at[leg, part],
            device_id=(lat, slab),
            device_id_type=MESH,
        )

    def to_y(leg, part, source, target, other):
        return along(source, target, y, leg, part, x * along_y + other)

    def to_x(leg, part, source, target, other):
        return along(source, target, x, leg, part, other * along_y + y)

    def wait_blocks(count, blocks, sem):
        for some in range(1, blocks.shape[0] + 1):

            @pl.when(count == some)
            def _(some=some):
                taken = blocks.at[pl.ds(0, some)]
                pltpu.make_async_copy(taken, taken, sem).wait()

    def start(copy):
        copy.start()

    steps = sorted(range(1, along_y), key=lambda step: -min(step, along_y - step))
    swapped = jnp.logical_not(first_band)
    turned = (ahead, swapped)

    def meet_along_y(part, act):
        for step in steps:
            other = (y + step) % along_y
            wanted = (x > 0) | ((other < y) & ((other > 0) | swapped))
            pl.when(wanted)(lambda other=other: act(to_y(0, part, sum_send.at[part], meet_y.at[part], other)))

    def meet_along_x(part, act):
        lax.fori_loop(
            0, x, lambda other, c: (act(to_x(0, part, sum_send.at[part], meet_x.at[part], other)), c)[1], 0
        )

    def far_along_x(part, act):
        begin = jnp.where(first_band & (y == 0), 1, 0)
        lax.fori_loop(
            begin, x, lambda other, c: (act(to_x(1, part, total_send.at[part], far_x.at[part], other)), c)[1], 0
        )

    def far_along_y(part, act):
        for step in steps:
            other = (y + step) % along_y
            act(to_y(1, part, pair_send.at[part, (y + step) // along_y], far_y.at[part], other))

    def to_first(act):
        @pl.when(first_band & (x == 0) & (y > 0))
        def _():
            for part in (0, 1):
                act(to_y(0, part, sum_send.at[part], meet_y.at[part], 0))

        @pl.when(first_band & (x > 0) & (y == 0))
        def _():
            for part in (0, 1):
                act(to_x(1, part, total_send.at[part], far_x.at[part], 0))

        pl.when(first_band & (lev > 0))(lambda: act(to_lower(0)))

    def to_lower(other):
        return pltpu.make_async_remote_copy(
            src_ref=late_send,
            dst_ref=late_recv.at[lev],
            send_sem=late_ssem.at[0],
            recv_sem=late_rsem.at[0],
            device_id=(lat, other),
            device_id_type=MESH,
        )

    def late_to_lower(act):
        lax.fori_loop(
            first_band.astype(jnp.int32), lev, lambda other, c: (act(to_lower(other)), c)[1], 0
        )

    pl.when(ahead)(lambda: (enter(), start_rest(), None)[-1])
    for part in (0, 1):
        pl.when(jnp.logical_not(turned[part]))(lambda part=part: meet_along_y(part, start))
        pl.when(turned[part])(lambda part=part: meet_along_x(part, start))

    @pl.when(lev > 0)
    def _():
        for side, interface in ((1, south_interface), (0, north_interface)):
            wait_halos(0, side)
            wait_halos(1, side)
            mine = 1 - side
            wind = spread(interface * 0.25) * (first_send[mine, 0] + first_recv[side, 0])
            flux = wind * (first_send[mine, 1] + first_recv[side, 1])
            late_send[side : side + 1] = jnp.sum(weights * flux, axis=0, keepdims=True)
            late_send[side + 2 : side + 3] = rows_recv[side, 0:1]
        late_to_lower(start)

    def second_along_x(part):
        wait_blocks(jnp.where(x > 0, along_y - 1, along_y - 1 - y), meet_y.at[part], sum_rsem.at[0, part])
        below, total_y = jnp.zeros((half, width), F32), sum_send[part]
        for step in range(1, along_y):
            other = (y + step) % along_y
            comes = (x > 0) | (other > y)
            came = jnp.where(comes, meet_y[part, other], 0.0)
            total_y += came
            below += jnp.where(other > y, came, 0.0)
        total_send[part] = total_y
        hold_ref[part] = below
        far_along_x(part, start)

    def second_along_y(part):
        wait_blocks(groups - 1 - x, meet_x.at[part], sum_rsem.at[0, part])

        def add(other, total):
            return total + meet_x[part, other]

        below = lax.fori_loop(x + 1, levs // along_y, add, jnp.zeros((half, width), F32))
        hold_ref[part] = below
        pair_send[part, 0] = below
        pair_send[part, 1] = below + sum_send[part]
        far_along_y(part, start)

    for part in (0, 1):
        pl.when(jnp.logical_not(turned[part]))(lambda part=part: second_along_x(part))
        pl.when(turned[part])(lambda part=part: second_along_y(part))

    @pl.when(first_band & (lev > 0))
    def _():
        pl.semaphore_wait(ready, 1)

    to_first(start)

    half_zonal = 0.5 * zonal_wide
    inner_upper = jnp.where(row_of < rows - 1, 0.25 * upper_wide, 0.0)

    def local(step, below):
        k = levels - 1 - step
        weight = w_ref[lev * levels + k]
        wind, cross = u_ref[k], v_ref[k]
        wind_full = wrapped(wind)
        wind_pair = 0.25 * (wind_full + east(wind_full))
        cross_pair = inner_upper * (cross + pltpu.roll(cross, rows - 1, 0))

        def moved(tracer):
            around = wrapped(tracer)
            flux = wind_pair * (around + east(around))
            change = (flux - west(flux, width))[:, :width]
            north = cross_pair * (tracer + pltpu.roll(tracer, rows - 1, 0))
            return tracer - zonal_wide * change - merid_wide * (north - pltpu.roll(north, 1, 0))

        heat, humid = moved(t_ref[k]), moved(q_ref[k])
        t_out[k] = heat
        q_out[k] = humid
        below = below + weight * (heat + MOIST_CORRECTION * humid)
        c_out[k] = below
        around = wrapped(below)
        u_out[k] = wind - half_zonal * (east(around) - west(around, width))[:, :width]
        north = jnp.where(row_of == rows - 1, 0.0, pltpu.roll(below, rows - 1, 0))
        south = jnp.where(row_of == 0, 0.0, pltpu.roll(below, 1, 0))
        v_out[k] = cross - 0.5 * MERID_RATE * (north - south)
        return below

    lax.fori_loop(0, levels, local, jnp.zeros((rows, width), F32), unroll=2)

    def from_below(value):
        reach = 1
        while reach < levels:
            lower_part = pltpu.roll(value, levels - reach, 0)
            value = value + jnp.where(level_wide + reach < levels, lower_part, 0.0)
            reach *= 2
        return value

    level_wide = lax.broadcasted_iota(jnp.int32, (levels, width), 0)

    @pl.when(lev == 0)
    def _():
        for side in (0, 1):
            wait_halos(0, side)
            wait_halos(1, side)

    for side in (0, 1):
        wait_halos(2, side)
    for side, exists, row, beside_row, interface, merid_edge, sign in (
        (0, has_north, rows - 1, rows - 2, north_interface, merid_north, 1.0),
        (1, has_south, 0, 1, south_interface, merid_south, -1.0),
    ):
        mine = 1 - side
        wind = spread(interface * 0.25) * (first_send[mine, 0] + first_recv[side, 0])
        heat_flux = wind * (rest_send[mine, 0] + rest_recv[side, 0])
        humid_flux = wind * (rest_send[mine, 1] + rest_recv[side, 1])
        out = sign * spread(merid[row : row + 1])
        t_out[:, row, :] = t_out[:, row, :] - out * heat_flux
        q_out[:, row, :] = q_out[:, row, :] - out * humid_flux
        flux = heat_flux + MOIST_CORRECTION * humid_flux
        edge = from_below(weights * out * flux)
        beyond = weights * (rest_recv[side, 2] + sign * spread(merid_edge) * flux)
        beyond = from_below(jnp.where(exists, beyond, 0.0))
        c_out[:, row, :] = c_out[:, row, :] - edge
        around = wrapped(edge)
        turn = (east(around) - west(around, width))[:, :width]
        u_out[:, row, :] = u_out[:, row, :] + 0.5 * spread(zonal[row : row + 1]) * turn
        across = 0.5 * MERID_RATE * sign
        v_out[:, row, :] = v_out[:, row, :] - across * beyond
        v_out[:, beside_row, :] = v_out[:, beside_row, :] + across * edge

    def last_along_x(part):
        wait_blocks(groups - 1 - x, far_x.at[part], sum_rsem.at[1, part])

        def add(other, total):
            return total + far_x[part, other]

        hold_ref[part] = lax.fori_loop(x + 1, levs // along_y, add, hold_ref[part])

    def last_along_y(part):
        wait_blocks(along_y - 1, far_y.at[part], sum_rsem.at[1, part])
        total = hold_ref[part]
        for step in range(1, along_y):
            other = (y + step) % along_y
            total += far_y[part, other]
        hold_ref[part] = total

    for part in (0, 1):
        pl.when(jnp.logical_not(turned[part]))(lambda part=part: last_along_x(part))
        pl.when(turned[part])(lambda part=part: last_along_y(part))
    total = g_ref[...] + jnp.concatenate([hold_ref[0], hold_ref[1]], axis=0)

    around = wrapped(total)
    b_out[0] = total
    b_out[1] = half_zonal * (east(around) - west(around, width))[:, :width]
    north = jnp.where(row_of == rows - 1, 0.0, pltpu.roll(total, rows - 1, 0))
    south = jnp.where(row_of == 0, 0.0, pltpu.roll(total, 1, 0))
    b_out[2] = 0.5 * MERID_RATE * (north - south)

    wait_blocks(levs - 1 - lev, late_recv, late_rsem.at[0])
    edges = [late_recv[slab] for slab in range(levs)]
    while len(edges) > 1:
        edges = [sum(edges[n + 1 : n + 2], edges[n]) for n in range(0, len(edges), 2)]
    edges = edges[0]
    for side, exists, row, beside_row, merid_edge, sign in (
        (0, has_north, rows - 1, rows - 2, merid_north, 1.0),
        (1, has_south, 0, 1, merid_south, -1.0),
    ):
        flux = edges[side : side + 1]
        change = -sign * merid_wide[row : row + 1] * flux
        beyond = rows_recv[side, 1:2] + edges[side + 2 : side + 3] + sign * widen(merid_edge, width) * flux
        around = wrapped(change)
        turn = (east(around) - west(around, width))[:, :width]
        across = 0.5 * MERID_RATE * sign
        b_out[0, row : row + 1] += change
        b_out[1, row : row + 1] += half_zonal[row : row + 1] * turn
        b_out[2, row : row + 1] += across * jnp.where(exists, beyond, 0.0)
        b_out[2, beside_row : beside_row + 1] += across * change

    sides = has_south.astype(jnp.int32) + has_north.astype(jnp.int32)
    for kind, send in enumerate((first_send, rows_send, rest_send)):
        wait_blocks(sides, send, halo_ssem.at[kind])
    for part in (0, 1):

        @pl.when(jnp.logical_not(turned[part]))
        def _(part=part):
            wait_blocks(jnp.where(x > 0, along_y - 1, y), meet_y.at[part], sum_ssem.at[0, part])
            wait_blocks(x, far_x.at[part], sum_ssem.at[1, part])

        @pl.when(turned[part])
        def _(part=part):
            wait_blocks(x, meet_x.at[part], sum_ssem.at[0, part])
            wait_blocks(along_y - 1, far_y.at[part], sum_ssem.at[1, part])

    wait_blocks(lev, late_recv, late_ssem.at[0])


def finish_kernel(t_in, q_in, u_in, v_in, c_in, b_in, t, q, u, v, h, u_new, v_new, h_new, sems):
    copies = [
        pltpu.make_async_copy(source, target, sems.at[n])
        for n, (source, target) in enumerate([(t_in, t), (q_in, q), (h_new, h), (u_new, u), (v_new, v)])
    ]
    copies[0].start()
    copies[1].start()
    for k in range(t_in.shape[0]):
        h_new[k] = c_in[k] + b_in[0]
    copies[2].start()
    for k in range(t_in.shape[0]):
        u_new[k] = u_in[k] - b_in[1]
    copies[3].start()
    for k in range(t_in.shape[0]):
        v_new[k] = v_in[k] - b_in[2]
    copies[4].start()
    for copy in copies:
        copy.wait()


def body(zonal, poleward, heat, humidity, ground, weights):
    levels, rows, width = heat.shape
    levs = lax.axis_size("lev")
    along_y = 4 if levs % 4 == 0 else levs
    along_x, half = levs // along_y, rows // 2
    slab = (levels, rows, width)
    anywhere = pl.BlockSpec(memory_space=pl.ANY)
    vmem = pl.BlockSpec(memory_space=pltpu.VMEM)
    dma = pltpu.SemaphoreType.DMA
    args = [pltpu.with_memory_space_constraint(x, pltpu.HBM) for x in (zonal, poleward, heat, humidity, ground, weights)]
    parts = pl.pallas_call(
        advect_kernel,
        name="advect",
        out_shape=[pltpu.VMEM(slab, F32)] * 5 + [pltpu.VMEM((3, rows, width), F32)],
        in_specs=[anywhere] * 6,
        out_specs=[vmem] * 6,
        scratch_shapes=[
            pltpu.VMEM((4,) + slab, F32),
            pltpu.VMEM((rows, width), F32),
            pltpu.SMEM(weights.shape, F32),
            pltpu.VMEM((4, 2, levels, 2, width), F32),
            pltpu.VMEM((2, 2, levels, width), F32),
            pltpu.VMEM((2, 2, levels, width), F32),
            pltpu.VMEM((2, 2, width), F32),
            pltpu.VMEM((2, 2, width), F32),
            pltpu.VMEM((2, 3, levels, width), F32),
            pltpu.VMEM((2, 3, levels, width), F32),
            pltpu.VMEM((2, half, width), F32),
            pltpu.VMEM((2, along_y, half, width), F32),
            pltpu.VMEM((2, half, width), F32),
            pltpu.VMEM((2, along_x, half, width), F32),
            pltpu.VMEM((2, along_x, half, width), F32),
            pltpu.VMEM((2, 2, half, width), F32),
            pltpu.VMEM((2, along_y, half, width), F32),
            pltpu.VMEM((2, half, width), F32),
            pltpu.VMEM((4, width), F32),
            pltpu.VMEM((levs, 4, width), F32),
            dma((4,)),
            dma((3,)),
            dma((3, 2)),
            dma((2, 2)),
            dma((2, 2)),
            dma((1,)),
            dma((1,)),
            pltpu.SemaphoreType.REGULAR,
        ],
        compiler_params=pltpu.CompilerParams(
            collective_id=0, has_side_effects=True, vmem_limit_bytes=32 * 2**20
        ),
    )(*args)
    return pl.pallas_call(
        finish_kernel,
        name="finish",
        out_shape=[jax.ShapeDtypeStruct(slab, F32)] * 5,
        in_specs=[vmem] * 6,
        out_specs=[anywhere] * 5,
        scratch_shapes=[pltpu.VMEM(slab, F32)] * 3 + [dma((5,))],
        compiler_params=pltpu.CompilerParams(vmem_limit_bytes=16 * 2**20),
    )(*parts)


def solution(mesh):
    slab = P("lev", "lat", None)
    return jax.shard_map(
        body,
        mesh=mesh,
        in_specs=(slab,) * 4 + (P("lat", None), P()),
        out_specs=(slab,) * 5,
        check_vma=False,
    )
```

```python
import functools
import jax
import jax.numpy as jnp
from jax import lax
from jax.experimental import pallas as pl
from jax.experimental.pallas import tpu as pltpu
from jax.sharding import PartitionSpec as P

ZONAL_RATE = 0.1
MERID_RATE = 0.25
POLAR_CAP = 0.2
MOIST_CORRECTION = 0.6
F32 = jnp.float32
MESH = pl.DeviceIdType.MESH


def lat_weights(row_index, circle_sum):
    spacing = jnp.pi / circle_sum
    middle_boxes = jnp.cos(-jnp.pi / 2 + (row_index + 0.5) * spacing)
    upper_interface = jnp.where(
        row_index + 1.0 < circle_sum, jnp.cos(-jnp.pi / 2 + (row_index + 1.0) * spacing), 0.0
    )
    lower_interface = jnp.where(row_index > 0.5, jnp.cos(-jnp.pi / 2 + row_index * spacing), 0.0)
    return middle_boxes, upper_interface, lower_interface


def widen(column, width):
    whole, rest = width // 128, width % 128
    parts = [column] * whole + ([column[:, :rest]] if rest else [])
    return jnp.concatenate(parts, axis=1)


def wrapped(value):
    width = value.shape[1]
    extra = -width % 128
    if extra == 0:
        return value
    return jnp.concatenate([value, value[:, :extra]], axis=1)


def east(full):
    return pltpu.roll(full, full.shape[1] - 1, 1)


def west(full, width):
    size = full.shape[1]
    rolled = pltpu.roll(full, 1, 1)
    if size == width:
        return rolled
    last = pltpu.roll(full[:, size - 128 :], 128 - (width - 1 - (size - 128)), 1)
    lane = lax.broadcasted_iota(jnp.int32, last.shape, 1)
    start = jnp.where(lane == 0, last, rolled[:, :128])
    return jnp.concatenate([start, rolled[:, 128:]], axis=1)


def advect_kernel(
    u_hbm, v_hbm, t_hbm, q_hbm, g_hbm, w_hbm,
    t_out, q_out, u_out, v_out, c_out, b_out,
    whole_ref, g_ref, w_ref, edge_rows,
    first_send, first_recv, rows_send, rows_recv, rest_send, rest_recv,
    sum_send, meet_y, total_send, far_x, meet_x, pair_send, far_y, hold_ref,
    late_send, late_recv,
    in_sem, halo_ssem, halo_rsem, sum_ssem, sum_rsem, late_ssem, late_rsem, ready,
):
    lat, lev = lax.axis_index("lat"), lax.axis_index("lev")
    lats, levs = lax.axis_size("lat"), lax.axis_size("lev")
    along_y = meet_y.shape[1]
    groups = levs // along_y
    x, y = lev // along_y, lev % along_y
    v_ref, t_ref, q_ref, u_ref = [whole_ref.at[kind] for kind in range(4)]
    levels, rows, width = t_ref.shape
    half = rows // 2
    circle_sum = rows * lats
    full = width + (-width % 128)
    has_south, has_north = lat > 0, lat < lats - 1

    barrier = pltpu.get_barrier_semaphore()
    first_band = lat == 0
    first = first_band & (lev == 0)

    def greet(band, slab):
        pl.semaphore_signal(barrier, inc=1, device_id=(band, slab), device_id_type=MESH)

    @pl.when(has_south)
    def _():
        greet(lat - 1, lev)

    @pl.when(has_north)
    def _():
        greet(lat + 1, lev)

    pl.when(first_band & (lev > 0))(lambda: greet(lat, 0))

    @pl.when(jnp.logical_not(first))
    def _():
        lax.fori_loop(lev + 1, levs, lambda slab, c: (greet(lat, slab), c)[1], 0)
        known = jnp.maximum(x * along_y, first_band.astype(jnp.int32))
        lax.fori_loop(known, lev, lambda slab, c: (greet(lat, slab), c)[1], 0)

    edge_loads = [
        pltpu.make_async_copy(
            source.at[:, pl.ds(side * (rows - 2), 2), :], edge_rows.at[kind, side], in_sem.at[2]
        )
        for kind, source in enumerate([v_hbm, t_hbm, q_hbm, u_hbm])
        for side in (0, 1)
    ]
    small_loads = [
        pltpu.make_async_copy(w_hbm, w_ref, in_sem.at[0]),
        pltpu.make_async_copy(g_hbm, g_ref, in_sem.at[1]),
    ]
    whole_loads = [
        pltpu.make_async_copy(source, whole_ref.at[kind], in_sem.at[3])
        for kind, source in enumerate([v_hbm, t_hbm, q_hbm, u_hbm])
    ]
    for load in edge_loads + small_loads:
        load.start()

    band = (lat * rows + lax.broadcasted_iota(jnp.int32, (rows, 128), 0)).astype(F32)
    centre, upper, lower = lat_weights(band, circle_sum)
    zonal = ZONAL_RATE / jnp.maximum(centre, POLAR_CAP)
    merid = MERID_RATE / centre
    beside = lat * rows - 1 + (rows + 1) * lax.broadcasted_iota(jnp.int32, (8, 128), 0)
    beside_centre, _, _ = lat_weights(beside.astype(F32), circle_sum)
    merid_beside = MERID_RATE / beside_centre
    south_interface, north_interface = lower[0:1], upper[rows - 1 :]
    merid_south, merid_north = merid_beside[0:1], merid_beside[1:2]
    row_of = lax.broadcasted_iota(jnp.int32, (rows, width), 0)
    upper_wide = widen(upper, width)
    zonal_wide, merid_wide = widen(zonal, width), widen(merid, width)

    def spread(row):
        return widen(jnp.broadcast_to(row, (levels, 128)), width)

    def clear(slab, carry):
        late_recv[slab] = jnp.zeros(late_recv.shape[1:], F32)
        return carry

    lax.fori_loop(0, lev + 1, clear, 0)

    for side, exists in ((0, has_north), (1, has_south)):

        @pl.when(jnp.logical_not(exists))
        def _(side=side):
            first_recv[side] = jnp.zeros(first_recv.shape[1:], F32)
            rows_recv[side] = jnp.zeros(rows_recv.shape[1:], F32)
            rest_recv[side] = jnp.zeros(rest_recv.shape[1:], F32)

    def halo(kind, send, recv, side):
        return pltpu.make_async_remote_copy(
            src_ref=send.at[side],
            dst_ref=recv.at[side],
            send_sem=halo_ssem.at[kind],
            recv_sem=halo_rsem.at[kind, side],
            device_id=(lat - 1 if side == 0 else lat + 1, lev),
            device_id_type=MESH,
        )

    halos = [
        [halo(kind, send, recv, side) for side in (0, 1)]
        for kind, (send, recv) in enumerate(
            [(first_send, first_recv), (rows_send, rows_recv), (rest_send, rest_recv)]
        )
    ]

    def start_halos(kind):
        pl.when(has_south)(halos[kind][0].start)
        pl.when(has_north)(halos[kind][1].start)

    def wait_halos(kind, side):
        pl.when(has_south if side == 1 else has_north)(halos[kind][side].wait_recv)

    pltpu.make_async_copy(edge_rows, edge_rows, in_sem.at[2]).wait()
    for load in whole_loads:
        load.start()

    def edge_row(kind, side, inner=False):
        return edge_rows[kind, side, :, side if not inner else 1 - side, :]

    for side in (0, 1):
        first_send[side, 0] = edge_row(0, side)
        first_send[side, 1] = edge_row(1, side) + MOIST_CORRECTION * edge_row(2, side)
    def enter():
        pl.semaphore_wait(
            barrier,
            jnp.where(first, levs - 1, lev - first_band.astype(jnp.int32) + along_y - 1 - y)
            + has_south.astype(jnp.int32)
            + has_north.astype(jnp.int32),
        )
        start_halos(0)

    ahead = lat % 2 == 1
    pl.when(jnp.logical_not(ahead))(enter)
    for load in small_loads:
        load.wait()
    level_of = lax.broadcasted_iota(jnp.int32, (levels, 128), 0)
    weights = jnp.zeros((levels, 128), F32)
    for k in range(levels):
        weights = jnp.where(level_of == k, w_ref[lev * levels + k], weights)
    weights = widen(weights, width)

    for side, row, interface, sign in (
        (0, 0, upper[0:1], -1.0),
        (1, rows - 1, lower[rows - 1 :], 1.0),
    ):
        tracer = first_send[side, 1]
        tracer_in = edge_row(1, side, True) + MOIST_CORRECTION * edge_row(2, side, True)
        flux_in = (
            spread(interface * 0.25)
            * (first_send[side, 0] + edge_row(0, side, True))
            * (tracer + tracer_in)
        )
        wind = wrapped(edge_row(3, side))
        around = wrapped(tracer)
        flux = 0.25 * (wind + east(wind)) * (around + east(around))
        change = (flux - west(flux, width))[:, :width]
        part = (
            tracer
            - spread(zonal[row : row + 1]) * change
            + sign * spread(merid[row : row + 1]) * flux_in
        )
        rest_send[side, 0] = edge_row(1, side)
        rest_send[side, 1] = edge_row(2, side)
        rest_send[side, 2] = part
        rows_send[side, 0:1] = jnp.sum(weights * part, axis=0, keepdims=True)
        rows_send[side, 1:2] = g_ref[row : row + 1, :]

    def start_rest():
        start_halos(1)
        start_halos(2)

        @pl.when(first)
        def _():
            def answer(slab, carry):
                pl.semaphore_signal(ready, inc=1, device_id=(lat, slab), device_id_type=MESH)
                return carry

            lax.fori_loop(1, levs, answer, 0)

    pl.when(jnp.logical_not(ahead))(start_rest)
    pltpu.make_async_copy(whole_ref, whole_ref, in_sem.at[3]).wait()

    def partial(k, carry):
        zonal_sum, merid_sum, own_sum = carry
        weight = w_ref[lev * levels + k]
        tracer = t_ref[k] + MOIST_CORRECTION * q_ref[k]
        around = wrapped(tracer)
        wind = wrapped(u_ref[k])
        zonal_sum += weight * ((wind + east(wind)) * (around + east(around)))
        cross = v_ref[k]
        merid_sum += weight * (
            (cross + pltpu.roll(cross, rows - 1, 0)) * (tracer + pltpu.roll(tracer, rows - 1, 0))
        )
        return zonal_sum, merid_sum, own_sum + weight * tracer

    zonal_sum, merid_sum, own_sum = lax.fori_loop(
        0,
        levels,
        partial,
        (jnp.zeros((rows, full), F32), jnp.zeros((rows, width), F32), jnp.zeros((rows, width), F32)),
        unroll=True,
    )
    north_sum = jnp.where(row_of < rows - 1, 0.25 * upper_wide * merid_sum, 0.0)
    slab_sum = (
        own_sum
        - zonal_wide * (0.25 * (zonal_sum - west(zonal_sum, width)))[:, :width]
        - merid_wide * (north_sum - pltpu.roll(north_sum, 1, 0))
    )

    sum_send[0] = slab_sum[:half]
    sum_send[1] = slab_sum[half:]

    def along(source, target, here, leg, part, slab):
        return pltpu.make_async_remote_copy(
            src_ref=source,
            dst_ref=target.at[here],
            send_sem=sum_ssem.at[leg, part],
            recv_sem=sum_rsem.at[leg, part],
            device_id=(lat, slab),
            device_id_type=MESH,
        )

    def to_y(leg, part, source, target, other):
        return along(source, target, y, leg, part, x * along_y + other)

    def to_x(leg, part, source, target, other):
        return along(source, target, x, leg, part, other * along_y + y)

    def wait_blocks(count, blocks, sem):
        for some in range(1, blocks.shape[0] + 1):

            @pl.when(count == some)
            def _(some=some):
                taken = blocks.at[pl.ds(0, some)]
                pltpu.make_async_copy(taken, taken, sem).wait()

    def start(copy):
        copy.start()

    steps = sorted(range(1, along_y), key=lambda step: -min(step, along_y - step))
    swapped = jnp.logical_not(first_band)
    turned = (ahead, swapped)

    def meet_along_y(part, act):
        for step in steps:
            other = (y + step) % along_y
            wanted = (x > 0) | ((other < y) & ((other > 0) | swapped))
            pl.when(wanted)(lambda other=other: act(to_y(0, part, sum_send.at[part], meet_y.at[part], other)))

    def meet_along_x(part, act):
        lax.fori_loop(
            0, x, lambda other, c: (act(to_x(0, part, sum_send.at[part], meet_x.at[part], other)), c)[1], 0
        )

    def far_along_x(part, act):
        begin = jnp.where(first_band & (y == 0), 1, 0)
        lax.fori_loop(
            begin, x, lambda other, c: (act(to_x(1, part, total_send.at[part], far_x.at[part], other)), c)[1], 0
        )

    def far_along_y(part, act):
        for step in steps:
            other = (y + step) % along_y
            act(to_y(1, part, pair_send.at[part, (y + step) // along_y], far_y.at[part], other))

    def to_first(act):
        @pl.when(first_band & (x == 0) & (y > 0))
        def _():
            for part in (0, 1):
                act(to_y(0, part, sum_send.at[part], meet_y.at[part], 0))

        @pl.when(first_band & (x > 0) & (y == 0))
        def _():
            for part in (0, 1):
                act(to_x(1, part, total_send.at[part], far_x.at[part], 0))

        pl.when(first_band & (lev > 0))(lambda: act(to_lower(0)))

    def to_lower(other):
        return pltpu.make_async_remote_copy(
            src_ref=late_send,
            dst_ref=late_recv.at[lev],
            send_sem=late_ssem.at[0],
            recv_sem=late_rsem.at[0],
            device_id=(lat, other),
            device_id_type=MESH,
        )

    def late_to_lower(act):
        lax.fori_loop(
            first_band.astype(jnp.int32), lev, lambda other, c: (act(to_lower(other)), c)[1], 0
        )

    pl.when(ahead)(lambda: (enter(), start_rest(), None)[-1])
    for part in (0, 1):
        pl.when(jnp.logical_not(turned[part]))(lambda part=part: meet_along_y(part, start))
        pl.when(turned[part])(lambda part=part: meet_along_x(part, start))

    @pl.when(lev > 0)
    def _():
        for side, interface in ((1, south_interface), (0, north_interface)):
            wait_halos(0, side)
            wait_halos(1, side)
            mine = 1 - side
            wind = spread(interface * 0.25) * (first_send[mine, 0] + first_recv[side, 0])
            flux = wind * (first_send[mine, 1] + first_recv[side, 1])
            late_send[side : side + 1] = jnp.sum(weights * flux, axis=0, keepdims=True)
            late_send[side + 2 : side + 3] = rows_recv[side, 0:1]
        late_to_lower(start)

    def second_along_x(part):
        wait_blocks(jnp.where(x > 0, along_y - 1, along_y - 1 - y), meet_y.at[part], sum_rsem.at[0, part])
        below, total_y = jnp.zeros((half, width), F32), sum_send[part]
        for step in range(1, along_y):
            other = (y + step) % along_y
            comes = (x > 0) | (other > y)
            came = jnp.where(comes, meet_y[part, other], 0.0)
            total_y += came
            below += jnp.where(other > y, came, 0.0)
        total_send[part] = total_y
        hold_ref[part] = below
        far_along_x(part, start)

    def second_along_y(part):
        wait_blocks(groups - 1 - x, meet_x.at[part], sum_rsem.at[0, part])

        def add(other, total):
            return total + meet_x[part, other]

        below = lax.fori_loop(x + 1, levs // along_y, add, jnp.zeros((half, width), F32))
        hold_ref[part] = below
        pair_send[part, 0] = below
        pair_send[part, 1] = below + sum_send[part]
        far_along_y(part, start)

    for part in (0, 1):
        pl.when(jnp.logical_not(turned[part]))(lambda part=part: second_along_x(part))
        pl.when(turned[part])(lambda part=part: second_along_y(part))

    @pl.when(first_band & (lev > 0))
    def _():
        pl.semaphore_wait(ready, 1)

    to_first(start)

    half_zonal = 0.5 * zonal_wide
    inner_upper = jnp.where(row_of < rows - 1, 0.25 * upper_wide, 0.0)

    def local(step, below):
        k = levels - 1 - step
        weight = w_ref[lev * levels + k]
        wind, cross = u_ref[k], v_ref[k]
        wind_full = wrapped(wind)
        wind_pair = 0.25 * (wind_full + east(wind_full))
        cross_pair = inner_upper * (cross + pltpu.roll(cross, rows - 1, 0))

        def moved(tracer):
            around = wrapped(tracer)
            flux = wind_pair * (around + east(around))
            change = (flux - west(flux, width))[:, :width]
            north = cross_pair * (tracer + pltpu.roll(tracer, rows - 1, 0))
            return tracer - zonal_wide * change - merid_wide * (north - pltpu.roll(north, 1, 0))

        heat, humid = moved(t_ref[k]), moved(q_ref[k])
        t_out[k] = heat
        q_out[k] = humid
        below = below + weight * (heat + MOIST_CORRECTION * humid)
        c_out[k] = below
        around = wrapped(below)
        u_out[k] = wind - half_zonal * (east(around) - west(around, width))[:, :width]
        north = jnp.where(row_of == rows - 1, 0.0, pltpu.roll(below, rows - 1, 0))
        south = jnp.where(row_of == 0, 0.0, pltpu.roll(below, 1, 0))
        v_out[k] = cross - 0.5 * MERID_RATE * (north - south)
        return below

    lax.fori_loop(0, levels, local, jnp.zeros((rows, width), F32), unroll=2)

    def from_below(value):
        reach = 1
        while reach < levels:
            lower_part = pltpu.roll(value, levels - reach, 0)
            value = value + jnp.where(level_wide + reach < levels, lower_part, 0.0)
            reach *= 2
        return value

    level_wide = lax.broadcasted_iota(jnp.int32, (levels, width), 0)

    @pl.when(lev == 0)
    def _():
        for side in (0, 1):
            wait_halos(0, side)
            wait_halos(1, side)

    for side in (0, 1):
        wait_halos(2, side)
    for side, exists, row, beside_row, interface, merid_edge, sign in (
        (0, has_north, rows - 1, rows - 2, north_interface, merid_north, 1.0),
        (1, has_south, 0, 1, south_interface, merid_south, -1.0),
    ):
        mine = 1 - side
        wind = spread(interface * 0.25) * (first_send[mine, 0] + first_recv[side, 0])
        heat_flux = wind * (rest_send[mine, 0] + rest_recv[side, 0])
        humid_flux = wind * (rest_send[mine, 1] + rest_recv[side, 1])
        out = sign * spread(merid[row : row + 1])
        t_out[:, row, :] = t_out[:, row, :] - out * heat_flux
        q_out[:, row, :] = q_out[:, row, :] - out * humid_flux
        flux = heat_flux + MOIST_CORRECTION * humid_flux
        edge = from_below(weights * out * flux)
        beyond = weights * (rest_recv[side, 2] + sign * spread(merid_edge) * flux)
        beyond = from_below(jnp.where(exists, beyond, 0.0))
        c_out[:, row, :] = c_out[:, row, :] - edge
        around = wrapped(edge)
        turn = (east(around) - west(around, width))[:, :width]
        u_out[:, row, :] = u_out[:, row, :] + 0.5 * spread(zonal[row : row + 1]) * turn
        across = 0.5 * MERID_RATE * sign
        v_out[:, row, :] = v_out[:, row, :] - across * beyond
        v_out[:, beside_row, :] = v_out[:, beside_row, :] + across * edge

    def last_along_x(part):
        wait_blocks(groups - 1 - x, far_x.at[part], sum_rsem.at[1, part])

        def add(other, total):
            return total + far_x[part, other]

        hold_ref[part] = lax.fori_loop(x + 1, levs // along_y, add, hold_ref[part])

    def last_along_y(part):
        wait_blocks(along_y - 1, far_y.at[part], sum_rsem.at[1, part])
        total = hold_ref[part]
        for step in range(1, along_y):
            other = (y + step) % along_y
            total += far_y[part, other]
        hold_ref[part] = total

    for part in (0, 1):
        pl.when(jnp.logical_not(turned[part]))(lambda part=part: last_along_x(part))
        pl.when(turned[part])(lambda part=part: last_along_y(part))
    total = g_ref[...] + jnp.concatenate([hold_ref[0], hold_ref[1]], axis=0)

    around = wrapped(total)
    b_out[0] = total
    b_out[1] = half_zonal * (east(around) - west(around, width))[:, :width]
    north = jnp.where(row_of == rows - 1, 0.0, pltpu.roll(total, rows - 1, 0))
    south = jnp.where(row_of == 0, 0.0, pltpu.roll(total, 1, 0))
    b_out[2] = 0.5 * MERID_RATE * (north - south)

    wait_blocks(levs - 1 - lev, late_recv, late_rsem.at[0])
    edges = [late_recv[slab] for slab in range(levs)]
    while len(edges) > 1:
        edges = [sum(edges[n + 1 : n + 2], edges[n]) for n in range(0, len(edges), 2)]
    edges = edges[0]
    for side, exists, row, beside_row, merid_edge, sign in (
        (0, has_north, rows - 1, rows - 2, merid_north, 1.0),
        (1, has_south, 0, 1, merid_south, -1.0),
    ):
        flux = edges[side : side + 1]
        change = -sign * merid_wide[row : row + 1] * flux
        beyond = rows_recv[side, 1:2] + edges[side + 2 : side + 3] + sign * widen(merid_edge, width) * flux
        around = wrapped(change)
        turn = (east(around) - west(around, width))[:, :width]
        across = 0.5 * MERID_RATE * sign
        b_out[0, row : row + 1] += change
        b_out[1, row : row + 1] += half_zonal[row : row + 1] * turn
        b_out[2, row : row + 1] += across * jnp.where(exists, beyond, 0.0)
        b_out[2, beside_row : beside_row + 1] += across * change

    sides = has_south.astype(jnp.int32) + has_north.astype(jnp.int32)
    for kind, send in enumerate((first_send, rows_send, rest_send)):
        wait_blocks(sides, send, halo_ssem.at[kind])
    for part in (0, 1):

        @pl.when(jnp.logical_not(turned[part]))
        def _(part=part):
            wait_blocks(jnp.where(x > 0, along_y - 1, y), meet_y.at[part], sum_ssem.at[0, part])
            wait_blocks(x, far_x.at[part], sum_ssem.at[1, part])

        @pl.when(turned[part])
        def _(part=part):
            wait_blocks(x, meet_x.at[part], sum_ssem.at[0, part])
            wait_blocks(along_y - 1, far_y.at[part], sum_ssem.at[1, part])

    wait_blocks(lev, late_recv, late_ssem.at[0])


def finish_kernel(t_in, q_in, u_in, v_in, c_in, b_in, t, q, u, v, h, u_new, v_new, h_new, sems):
    copies = [
        pltpu.make_async_copy(source, target, sems.at[n])
        for n, (source, target) in enumerate([(t_in, t), (q_in, q), (h_new, h), (u_new, u), (v_new, v)])
    ]
    copies[0].start()
    copies[1].start()
    for k in range(t_in.shape[0]):
        h_new[k] = c_in[k] + b_in[0]
    copies[2].start()
    for k in range(t_in.shape[0]):
        u_new[k] = u_in[k] - b_in[1]
    copies[3].start()
    for k in range(t_in.shape[0]):
        v_new[k] = v_in[k] - b_in[2]
    copies[4].start()
    for copy in copies:
        copy.wait()


def body(zonal, poleward, heat, humidity, ground, weights):
    levels, rows, width = heat.shape
    levs = lax.axis_size("lev")
    along_y = 4 if levs % 4 == 0 else levs
    along_x, half = levs // along_y, rows // 2
    slab = (levels, rows, width)
    anywhere = pl.BlockSpec(memory_space=pl.ANY)
    vmem = pl.BlockSpec(memory_space=pltpu.VMEM)
    dma = pltpu.SemaphoreType.DMA
    args = [pltpu.with_memory_space_constraint(x, pltpu.HBM) for x in (zonal, poleward, heat, humidity, ground, weights)]
    parts = pl.pallas_call(
        advect_kernel,
        name="advect",
        out_shape=[pltpu.VMEM(slab, F32)] * 5 + [pltpu.VMEM((3, rows, width), F32)],
        in_specs=[anywhere] * 6,
        out_specs=[vmem] * 6,
        scratch_shapes=[
            pltpu.VMEM((4,) + slab, F32),
            pltpu.VMEM((rows, width), F32),
            pltpu.SMEM(weights.shape, F32),
            pltpu.VMEM((4, 2, levels, 2, width), F32),
            pltpu.VMEM((2, 2, levels, width), F32),
            pltpu.VMEM((2, 2, levels, width), F32),
            pltpu.VMEM((2, 2, width), F32),
            pltpu.VMEM((2, 2, width), F32),
            pltpu.VMEM((2, 3, levels, width), F32),
            pltpu.VMEM((2, 3, levels, width), F32),
            pltpu.VMEM((2, half, width), F32),
            pltpu.VMEM((2, along_y, half, width), F32),
            pltpu.VMEM((2, half, width), F32),
            pltpu.VMEM((2, along_x, half, width), F32),
            pltpu.VMEM((2, along_x, half, width), F32),
            pltpu.VMEM((2, 2, half, width), F32),
            pltpu.VMEM((2, along_y, half, width), F32),
            pltpu.VMEM((2, half, width), F32),
            pltpu.VMEM((4, width), F32),
            pltpu.VMEM((levs, 4, width), F32),
            dma((4,)),
            dma((3,)),
            dma((3, 2)),
            dma((2, 2)),
            dma((2, 2)),
            dma((1,)),
            dma((1,)),
            pltpu.SemaphoreType.REGULAR,
        ],
        compiler_params=pltpu.CompilerParams(
            collective_id=0, has_side_effects=True, vmem_limit_bytes=32 * 2**20
        ),
    )(*args)
    return pl.pallas_call(
        finish_kernel,
        name="finish",
        out_shape=[jax.ShapeDtypeStruct(slab, F32)] * 5,
        in_specs=[vmem] * 6,
        out_specs=[anywhere] * 5,
        scratch_shapes=[pltpu.VMEM(slab, F32)] * 3 + [dma((5,))],
        compiler_params=pltpu.CompilerParams(vmem_limit_bytes=16 * 2**20),
    )(*parts)


def solution(mesh):
    slab = P("lev", "lat", None)
    return jax.shard_map(
        body,
        mesh=mesh,
        in_specs=(slab,) * 4 + (P("lat", None), P()),
        out_specs=(slab,) * 5,
        check_vma=False,
    )
```
